512 devices in a mesh: space: 128 (over x, z, core), view: 4 (over y).
Axes of the slice: x: 4, y: 4, z: 16, core: 2. Of those that a mesh axis runs over, the one named last changes fastest.
Arguments:
- centers: float32 [3, 2097152], P(None, ('space', 'view')), may hold values from -13 to 13, as said below
- log_scales: float32 [3, 2097152], P(None, ('space', 'view')), may hold values from -5 to -3
- rotations: float32 [4, 2097152], P(None, ('space', 'view')), may hold values from 0.1 to 1.9
- opacity: float32 [2097152], P(('space', 'view')), may hold values from -1 to 6
- harmonics: float32 [3, 16, 2097152], P(None, None, ('space', 'view')), may hold values from -1.8 to 1.8
- cameras: float32 [4, 3], replicated, may hold values from -0.05 to 0.05
- send_index: int32 [128, 4, 128, 2], P('space', 'view'), may hold values from 0 to 4095, as said below
- tile_lists: int32 [128, 8, 128], P('space'), may hold values from 0 to 1023, as said below
- counts: int32 [128, 8], P('space'), may hold values from 32 to 128, as said below
- target: float32 [4, 3, 2048, 128], P('view', None, 'space'), may hold values from 0 to 1
Outputs:
- rendered: float32 [4, 3, 2048, 128], P('view', None, 'space')
- inverse_depth: float32 [4, 2048, 128], P('view', 'space')
- grad_centers: float32 [3, 2097152], P(None, ('space', 'view'))
- grad_scales: float32 [3, 2097152], P(None, ('space', 'view'))
- grad_rotations: float32 [4, 2097152], P(None, ('space', 'view'))
- grad_opacity: float32 [2097152], P(('space', 'view'))
- grad_harmonics: float32 [3, 16, 2097152], P(None, None, ('space', 'view'))
The draws below stay inside these ranges and needn't reach their ends.
Inputs may be any that keep to these rules, and one draw needn't show every extreme that they name: `send_index`: for each owner (first two indices) the 256 entries are distinct local Gaussian numbers. `tile_lists`: for each strip the 8 lists together name every slot exactly once; a list's Gaussians come front to back in every view. `counts`: some tile has all 128 entries live. `centers`: the third row (depth) lies from 2 to 6.
All inputs are finite; a program needn't handle non-finite values.
Results may differ from the reference program's by a relative error of at most 0.0003.
Values sent between devices are 32-bit elements; how exact they have to be, the bound alone decides.
A program may use at most 64 MiB of HBM per device.

```python
import math
import jax
import jax.numpy as jnp
from jax import lax

TILE = 16
TILES_DEV = 8
K = 128
G_DEV = 4096
SH_COEF = 16
STRIPS = 128
VIEWS = 4
SLOTS = 1024
CAP = 2
H = 2048
W = 128
GAUSS = 2097152


FOCAL_LENGTH = 512.0


def routing(key):
    owners = STRIPS * VIEWS
    subkeys = jax.random.split(jax.random.fold_in(key, 101), owners)
    send_order = jax.vmap(lambda subkey: jax.random.permutation(subkey, G_DEV))(subkeys).astype(jnp.int32)
    strip_keys = jax.random.split(jax.random.fold_in(key, 202), STRIPS)
    tile_order = jax.vmap(lambda subkey: jax.random.permutation(subkey, SLOTS))(strip_keys).astype(jnp.int32)
    return (send_order, tile_order)


def draw_send_index(key, part):
    send_order, tile_order = routing(key)
    key = jax.random.fold_in(key, 3)
    return send_order[:, :STRIPS * CAP].reshape(STRIPS, VIEWS, STRIPS, CAP)


def draw_tile_lists(key, part):
    send_order, tile_order = routing(key)
    key = jax.random.fold_in(key, 5)
    return tile_order.reshape(STRIPS, TILES_DEV, K)


def draw_counts(key, part):
    key = jax.random.fold_in(key, 7)
    level_key, count_key, spot_key = jax.random.split(key, 3)
    level = jax.random.randint(level_key, (STRIPS,), 0, 3)
    ceiling = jnp.array([K // 2, 3 * K // 4, K], dtype=jnp.int32)[level]
    drawn = jax.random.randint(count_key, (STRIPS, TILES_DEV), K // 4, ceiling[:, None] + 1)
    spot = jax.random.randint(spot_key, (), 0, STRIPS * TILES_DEV)
    flat_ids = jnp.arange(STRIPS * TILES_DEV).reshape(STRIPS, TILES_DEV)
    return jnp.where(flat_ids == spot, K, drawn).astype(jnp.int32)


def draw_centers(key, part):
    send_order, tile_order = routing(key)
    key = jax.random.fold_in(key, 9)
    owners = STRIPS * VIEWS
    sent_count = STRIPS * CAP
    owner_ids = jnp.arange(owners)[:, None]
    position = jnp.zeros((owners, G_DEV), jnp.int32).at[owner_ids, send_order].set(jnp.arange(G_DEV, dtype=jnp.int32)[None, :])
    strip_ids = jnp.arange(STRIPS)[:, None]
    inverse_tile = jnp.zeros((STRIPS, SLOTS), jnp.int32).at[strip_ids, tile_order].set(jnp.arange(SLOTS, dtype=jnp.int32)[None, :])
    is_sent = position < sent_count
    destination = jnp.minimum(position // CAP, STRIPS - 1)
    within = position % CAP
    owner_strip = owner_ids // VIEWS
    owner_view = owner_ids % VIEWS
    slot_number = (owner_view * STRIPS + owner_strip) * CAP + within
    list_place = inverse_tile[destination, slot_number]
    home_tile = list_place // K
    list_rank = list_place % K
    keys_six = jax.random.split(key, 6)
    shape = (owners, G_DEV)
    row_inside = jax.random.uniform(keys_six[0], shape, jnp.float32, 0.5, TILE - 0.5)
    column_inside = jax.random.uniform(keys_six[1], shape, jnp.float32, 0.5, TILE - 0.5)
    fraction = jax.random.uniform(keys_six[2], shape, jnp.float32, 0.0, 1.0)
    row_home = destination.astype(jnp.float32) * TILE + row_inside
    column_home = home_tile.astype(jnp.float32) * TILE + column_inside
    depth_home = 2.0 + 4.0 * (list_rank.astype(jnp.float32) + fraction) / K
    row_free = jax.random.uniform(keys_six[3], shape, jnp.float32, 0.0, H)
    column_free = jax.random.uniform(keys_six[4], shape, jnp.float32, 0.0, W)
    depth_free = jax.random.uniform(keys_six[5], shape, jnp.float32, 2.0, 6.0)
    row_value = jnp.where(is_sent, row_home, row_free)
    column_value = jnp.where(is_sent, column_home, column_free)
    depth = jnp.where(is_sent, depth_home, depth_free)
    world_x = (column_value - 0.5 * W) * depth / FOCAL_LENGTH
    world_y = (row_value - 0.5 * H) * depth / FOCAL_LENGTH
    return jnp.stack([world_x, world_y, depth]).reshape(3, owners * G_DEV).astype(jnp.float32)


def shard_levels(key, shape, shards, smallest, high):
    loudness = 1.0
    for axis_at, shards_of in shards:
        draws = jax.random.uniform(jax.random.fold_in(jax.random.fold_in(key, 6), axis_at), (shards_of,), jnp.float32, smallest / len(shards), high / len(shards))
        loudness = loudness * jnp.repeat(jnp.exp(draws), shape[axis_at] // shards_of).reshape((-1,) + (1,) * (len(shape) - 1 - axis_at))
    return loudness


def normal_values(stream_key, dims, scale, bound, shards=(), kind=jnp.bfloat16):
    values = jax.random.normal(stream_key, dims, jnp.float32) * scale
    if len(shards) > 0:
        values = shard_levels(stream_key, dims, shards, -0.22, 0.18) * values
    return jnp.clip(values, min=-bound, max=bound).astype(kind)


def setup_inputs(seed: int = 0) -> dict:
    streams_of = jax.random.split(jax.random.key(seed), 11)
    return {
        "centers": draw_centers(jax.random.fold_in(streams_of[10], 71), 0),
        "log_scales": jnp.clip(-5.0 + 2.0 * jax.random.uniform(streams_of[1], (3, GAUSS), jnp.float32) ** shard_levels(streams_of[1], (3, GAUSS), ((1, 512),), -0.2, 0.2), -5.0, -3.0),
        "rotations": jnp.clip(1.0 + 0.18 * jax.random.normal(streams_of[2], (4, GAUSS), jnp.float32), 0.1, 1.9),
        "opacity": jnp.clip(-1.0 + 7.0 * jax.random.uniform(streams_of[3], (GAUSS,), jnp.float32) ** shard_levels(streams_of[3], (GAUSS,), ((0, 512),), -0.2, 0.2), -1.0, 6.0),
        "harmonics": normal_values(streams_of[4], (3, SH_COEF, GAUSS), 0.3, 1.8, ((2, 512),), jnp.float32),
        "cameras": jnp.clip(jax.random.uniform(streams_of[5], (VIEWS, 3), jnp.float32, -0.05, 0.05), -0.05, 0.05),
        "send_index": draw_send_index(jax.random.fold_in(streams_of[10], 71), 0),
        "tile_lists": draw_tile_lists(jax.random.fold_in(streams_of[10], 71), 0),
        "counts": draw_counts(jax.random.fold_in(streams_of[10], 71), 0),
        "target": jnp.clip(1.0 * jax.random.uniform(streams_of[9], (VIEWS, 3, H, W), jnp.float32) ** shard_levels(streams_of[9], (VIEWS, 3, H, W), ((0, 4), (2, 128)), -0.2, 0.2), 0.0, 1.0),
    }


FOCAL_LENGTH = 512.0
LOW_PASS = 0.3
ALPHA_MAX = 0.99
SMOOTHING = 0.05
STRUCTURE_WEIGHT = 0.2
STABLE_MEAN = 0.0001
STABLE_SPREAD = 0.0009
HARMONIC_ZERO = 0.28209479177387814
HARMONIC_ONE = 0.4886025119029199
HARMONIC_TWO = [1.0925484305920792, -1.0925484305920792, 0.31539156525252005, -1.0925484305920792, 0.5462742152960396]
HARMONIC_THREE = [-0.5900435899266435, 2.890611442640554, -0.4570457994644658, 0.3731763325901154, -0.4570457994644658, 1.445305721320277, -0.5900435899266435]
TAPS_RAW = [math.exp(-(offset - 5) ** 2 / 4.5) for offset in range(11)]
WINDOW_TAPS = [value / sum(TAPS_RAW) for value in TAPS_RAW]

def harmonic_basis(unit_x, unit_y, unit_z):
    square_x = unit_x * unit_x
    square_y = unit_y * unit_y
    square_z = unit_z * unit_z
    terms = [HARMONIC_ZERO * jnp.ones_like(unit_x), -HARMONIC_ONE * unit_y, HARMONIC_ONE * unit_z, -HARMONIC_ONE * unit_x, HARMONIC_TWO[0] * unit_x * unit_y, HARMONIC_TWO[1] * unit_y * unit_z, HARMONIC_TWO[2] * (2.0 * square_z - square_x - square_y), HARMONIC_TWO[3] * unit_x * unit_z, HARMONIC_TWO[4] * (square_x - square_y), HARMONIC_THREE[0] * unit_y * (3.0 * square_x - square_y), HARMONIC_THREE[1] * unit_x * unit_y * unit_z, HARMONIC_THREE[2] * unit_y * (4.0 * square_z - square_x - square_y), HARMONIC_THREE[3] * unit_z * (2.0 * square_z - 3.0 * square_x - 3.0 * square_y), HARMONIC_THREE[4] * unit_x * (4.0 * square_z - square_x - square_y), HARMONIC_THREE[5] * unit_z * (square_x - square_y), HARMONIC_THREE[6] * unit_x * (square_x - 3.0 * square_y)]
    return jnp.stack(terms)

def project_view(centers, log_scales, rotations, opacity, harmonics, camera, height, columns):
    shift_x = centers[0] - camera[0]
    shift_y = centers[1] - camera[1]
    shift_z = centers[2] - camera[2]
    inverse_z = 1.0 / shift_z
    pixel_column = FOCAL_LENGTH * shift_x * inverse_z + 0.5 * columns
    pixel_row = FOCAL_LENGTH * shift_y * inverse_z + 0.5 * height
    scalar_w, axis_x, axis_y, axis_z = (rotations[0], rotations[1], rotations[2], rotations[3])
    rot_scale = 2.0 / (scalar_w * scalar_w + axis_x * axis_x + axis_y * axis_y + axis_z * axis_z)
    rotation = [[1.0 - rot_scale * (axis_y * axis_y + axis_z * axis_z), rot_scale * (axis_x * axis_y - scalar_w * axis_z), rot_scale * (axis_x * axis_z + scalar_w * axis_y)], [rot_scale * (axis_x * axis_y + scalar_w * axis_z), 1.0 - rot_scale * (axis_x * axis_x + axis_z * axis_z), rot_scale * (axis_y * axis_z - scalar_w * axis_x)], [rot_scale * (axis_x * axis_z - scalar_w * axis_y), rot_scale * (axis_y * axis_z + scalar_w * axis_x), 1.0 - rot_scale * (axis_x * axis_x + axis_y * axis_y)]]
    scales = jnp.exp(log_scales)
    factor = [[rotation[first_axis][second_axis] * scales[second_axis] for second_axis in range(3)] for first_axis in range(3)]

    def product_entry(left_axis, right_axis):
        return factor[left_axis][0] * factor[right_axis][0] + factor[left_axis][1] * factor[right_axis][1] + factor[left_axis][2] * factor[right_axis][2]
    sigma_xx = product_entry(0, 0)
    sigma_xy = product_entry(0, 1)
    sigma_xz = product_entry(0, 2)
    sigma_yy = product_entry(1, 1)
    sigma_yz = product_entry(1, 2)
    sigma_zz = product_entry(2, 2)
    jacobian_a = FOCAL_LENGTH * inverse_z
    jacobian_x = -FOCAL_LENGTH * shift_x * inverse_z * inverse_z
    jacobian_y = -FOCAL_LENGTH * shift_y * inverse_z * inverse_z
    plane_a = jacobian_a * jacobian_a * sigma_xx + 2.0 * jacobian_a * jacobian_x * sigma_xz + jacobian_x * jacobian_x * sigma_zz + LOW_PASS
    plane_b = jacobian_a * jacobian_a * sigma_xy + jacobian_a * jacobian_y * sigma_xz + jacobian_x * jacobian_a * sigma_yz + jacobian_x * jacobian_y * sigma_zz
    plane_c = jacobian_a * jacobian_a * sigma_yy + 2.0 * jacobian_a * jacobian_y * sigma_yz + jacobian_y * jacobian_y * sigma_zz + LOW_PASS
    determinant = plane_a * plane_c - plane_b * plane_b
    conic_a = plane_c / determinant
    conic_b = -plane_b / determinant
    conic_c = plane_a / determinant
    opaque = jax.nn.sigmoid(opacity)
    length = jnp.sqrt(shift_x * shift_x + shift_y * shift_y + shift_z * shift_z)
    basis = harmonic_basis(shift_x / length, shift_y / length, shift_z / length)
    colors = jnp.maximum(0.0, 0.5 + lax.optimization_barrier(jnp.sum(harmonics * basis[None], axis=1)))
    return jnp.stack([pixel_column, pixel_row, conic_a, conic_b, conic_c, opaque, colors[0], colors[1], colors[2], inverse_z])

def render_tiles(gathered, live_count, strip_number):
    tile_count = gathered.shape[1]
    list_length = gathered.shape[2]
    pixel_ids = jnp.arange(TILE * TILE).astype(jnp.int32)
    tile_ids = jnp.arange(tile_count).astype(jnp.int32)
    pixel_x = (tile_ids[:, None] * TILE + pixel_ids[None, :] % TILE).astype(jnp.float32) + 0.5
    pixel_y = (strip_number * TILE + pixel_ids // TILE).astype(jnp.float32) + 0.5
    delta_x = gathered[0][:, None, :] - pixel_x[:, :, None]
    delta_y = gathered[1][:, None, :] - pixel_y[None, :, None]
    power = -0.5 * (gathered[2][:, None, :] * delta_x * delta_x + gathered[4][:, None, :] * delta_y * delta_y) - gathered[3][:, None, :] * delta_x * delta_y
    live_mask = (jnp.arange(list_length)[None, :] < live_count[:, None]).astype(jnp.float32)
    alphas = jnp.minimum(ALPHA_MAX, gathered[5][:, None, :] * jnp.exp(power)) * live_mask[:, None, :]
    log_keep = jnp.log(1.0 - alphas)
    log_trans = jnp.cumsum(log_keep, axis=-1) - log_keep
    weight = alphas * jnp.exp(log_trans)
    result = jnp.einsum('tpk,ftk->ftp', weight, gathered[6:10], precision=lax.Precision.HIGHEST)
    result = result.reshape(4, tile_count, TILE, TILE).transpose(0, 2, 1, 3)
    return result.reshape(4, TILE, tile_count * TILE)

def window_blur(stack_in, rows_out):
    vertical = WINDOW_TAPS[0] * stack_in[..., 0:rows_out, :]
    for offset in range(1, 11):
        vertical = vertical + WINDOW_TAPS[offset] * stack_in[..., offset:offset + rows_out, :]
    columns = stack_in.shape[-1]
    padded = jnp.pad(vertical, [(0, 0)] * (vertical.ndim - 1) + [(5, 5)])
    result = WINDOW_TAPS[0] * padded[..., 0:columns]
    for offset in range(1, 11):
        result = result + WINDOW_TAPS[offset] * padded[..., offset:offset + columns]
    return result

def structure_map(padded_x, padded_y, rows_out):
    stacked = jnp.stack([padded_x, padded_y, padded_x * padded_x, padded_y * padded_y, padded_x * padded_y])
    blurred = window_blur(stacked, rows_out)
    mean_x, mean_y, second_x, second_y, second_xy = (blurred[0], blurred[1], blurred[2], blurred[3], blurred[4])
    spread_x = second_x - mean_x * mean_x
    spread_y = second_y - mean_y * mean_y
    spread_xy = second_xy - mean_x * mean_y
    upper_part = (2.0 * mean_x * mean_y + STABLE_MEAN) * (2.0 * spread_xy + STABLE_SPREAD)
    lower_part = (mean_x * mean_x + mean_y * mean_y + STABLE_MEAN) * (spread_x + spread_y + STABLE_SPREAD)
    return upper_part / lower_part

def reference(centers, log_scales, rotations, opacity, harmonics, cameras, send_index, tile_lists, counts, target):
    height = TILE * STRIPS
    columns = TILE * TILES_DEV
    owner_base = ((jnp.arange(STRIPS)[:, None] * VIEWS + jnp.arange(VIEWS)[None, :]) * G_DEV).astype(jnp.int32)
    global_ids = send_index + owner_base[:, :, None, None]
    slot_ids = jnp.transpose(global_ids, (2, 1, 0, 3)).reshape(STRIPS, SLOTS)
    tile_gaussians = jax.vmap(lambda slot_row, list_rows: slot_row[list_rows])(slot_ids, tile_lists)

    def forward(centers, log_scales, rotations, opacity, harmonics):
        features = jax.vmap(lambda camera: project_view(centers, log_scales, rotations, opacity, harmonics, camera, height, columns))(cameras)

        def render_one(flat_index):
            view_number = flat_index // STRIPS
            strip_number = flat_index % STRIPS
            view_features = features[view_number]
            gathered = jnp.take(view_features, tile_gaussians[strip_number], axis=1)
            return render_tiles(gathered, counts[strip_number], strip_number)
        stacked = lax.map(jax.checkpoint(render_one), jnp.arange(VIEWS * STRIPS).astype(jnp.int32))
        stacked = stacked.reshape(VIEWS, STRIPS, 4, TILE, columns).transpose(0, 2, 1, 3, 4).reshape(VIEWS, 4, height, columns)
        rendered = stacked[:, :3]
        inverse_depth = stacked[:, 3]
        padding = ((0, 0), (0, 0), (5, 5), (0, 0))
        structure = structure_map(jnp.pad(rendered, padding), jnp.pad(target, padding), height)
        smooth = jnp.sqrt((rendered - target) ** 2 + SMOOTHING ** 2)
        loss_value = (jnp.sum((1.0 - STRUCTURE_WEIGHT) * smooth) + STRUCTURE_WEIGHT * jnp.sum(1.0 - structure)) / (TILE * TILE)
        return (loss_value, (rendered, inverse_depth))
    loss_value, pull_back, images = jax.vjp(forward, centers, log_scales, rotations, opacity, harmonics, has_aux=True)
    grads = pull_back(jnp.ones_like(loss_value))
    return (images[0], images[1], grads[0], grads[1], grads[2], grads[3], grads[4])
```

```python
import functools
import math

import jax
import jax.numpy as jnp
from jax import lax
from jax.experimental import pallas as pl
from jax.experimental.pallas import tpu as pltpu
from jax.sharding import PartitionSpec as P

TILE = 16
FOCAL_LENGTH = 512.0
LOW_PASS = 0.3
ALPHA_MAX = 0.99
SMOOTHING = 0.05
STRUCTURE_WEIGHT = 0.2
STABLE_MEAN = 0.0001
STABLE_SPREAD = 0.0009
HARMONIC_ZERO = 0.28209479177387814
HARMONIC_ONE = 0.4886025119029199
HARMONIC_TWO = [
    1.0925484305920792,
    -1.0925484305920792,
    0.31539156525252005,
    -1.0925484305920792,
    0.5462742152960396,
]
HARMONIC_THREE = [
    -0.5900435899266435,
    2.890611442640554,
    -0.4570457994644658,
    0.3731763325901154,
    -0.4570457994644658,
    1.445305721320277,
    -0.5900435899266435,
]
TAPS_RAW = [math.exp(-((offset - 5) ** 2) / 4.5) for offset in range(11)]
WINDOW_TAPS = [value / sum(TAPS_RAW) for value in TAPS_RAW]

F32 = jnp.float32
BF16 = jnp.bfloat16
MESH = pl.DeviceIdType.MESH
VMEM = pltpu.VMEM
EXACT = lax.Precision.HIGHEST


def harmonic_basis(ux, uy, uz):
    xx, yy, zz = ux * ux, uy * uy, uz * uz
    return [
        HARMONIC_ZERO * jnp.ones_like(ux),
        -HARMONIC_ONE * uy,
        HARMONIC_ONE * uz,
        -HARMONIC_ONE * ux,
        HARMONIC_TWO[0] * ux * uy,
        HARMONIC_TWO[1] * uy * uz,
        HARMONIC_TWO[2] * (2.0 * zz - xx - yy),
        HARMONIC_TWO[3] * ux * uz,
        HARMONIC_TWO[4] * (xx - yy),
        HARMONIC_THREE[0] * uy * (3.0 * xx - yy),
        HARMONIC_THREE[1] * ux * uy * uz,
        HARMONIC_THREE[2] * uy * (4.0 * zz - xx - yy),
        HARMONIC_THREE[3] * uz * (2.0 * zz - 3.0 * xx - 3.0 * yy),
        HARMONIC_THREE[4] * ux * (4.0 * zz - xx - yy),
        HARMONIC_THREE[5] * uz * (xx - yy),
        HARMONIC_THREE[6] * ux * (xx - 3.0 * yy),
    ]


def project(harmonics, center, log_scale, quaternion, opacity, camera, height, columns):
    tx, ty, tz = (center[i] - camera[i] for i in range(3))
    iz = 1.0 / tz
    u = FOCAL_LENGTH * tx * iz + 0.5 * columns
    r = FOCAL_LENGTH * ty * iz + 0.5 * height
    qw, qx, qy, qz = quaternion
    s = 2.0 / (qw * qw + qx * qx + qy * qy + qz * qz)
    rot = [
        [1.0 - s * (qy * qy + qz * qz), s * (qx * qy - qw * qz), s * (qx * qz + qw * qy)],
        [s * (qx * qy + qw * qz), 1.0 - s * (qx * qx + qz * qz), s * (qy * qz - qw * qx)],
        [s * (qx * qz - qw * qy), s * (qy * qz + qw * qx), 1.0 - s * (qx * qx + qy * qy)],
    ]
    scales = [jnp.exp(v) for v in log_scale]
    m = [[rot[i][j] * scales[j] for j in range(3)] for i in range(3)]

    def entry(i, j):
        return m[i][0] * m[j][0] + m[i][1] * m[j][1] + m[i][2] * m[j][2]

    ja = FOCAL_LENGTH * iz
    jx = -FOCAL_LENGTH * tx * iz * iz
    jy = -FOCAL_LENGTH * ty * iz * iz
    sxz, syz, szz = entry(0, 2), entry(1, 2), entry(2, 2)
    pa = ja * ja * entry(0, 0) + 2.0 * ja * jx * sxz + jx * jx * szz + LOW_PASS
    pb = ja * ja * entry(0, 1) + ja * jy * sxz + jx * ja * syz + jx * jy * szz
    pc = ja * ja * entry(1, 1) + 2.0 * ja * jy * syz + jy * jy * szz + LOW_PASS
    det = pa * pc - pb * pb
    opaque = 1.0 / (1.0 + jnp.exp(-opacity))
    length = jnp.sqrt(tx * tx + ty * ty + tz * tz)
    basis = harmonic_basis(tx / length, ty / length, tz / length)
    colors = []
    for ch in range(3):
        total = harmonics[ch * 16] * basis[0]
        for i in range(1, 16):
            total = total + harmonics[ch * 16 + i] * basis[i]
        colors.append(jnp.maximum(0.0, 0.5 + total))
    return [u, r, pc / det, -pb / det, pa / det, opaque, colors[0], colors[1], colors[2], iz]


def iota(shape, dim):
    return lax.broadcasted_iota(jnp.int32, shape, dim)


def one_hot(condition):
    return jnp.where(condition, 1.0, 0.0).astype(BF16)


def split(value, parts):
    out = []
    for _ in range(parts - 1):
        high = value.astype(BF16)
        out.append(high)
        value = value - high.astype(F32)
    out.append(value.astype(BF16))
    return out


def dot(a, b):
    return jnp.dot(a, b, preferred_element_type=F32)


def dot_exact(a, b):
    return jnp.dot(a, b, preferred_element_type=F32, precision=EXACT)


def view_camera(cam_ref):
    view = iota((8, 128), 0) // 2
    out = []
    for i in range(3):
        value = jnp.full((8, 128), cam_ref[3, i], F32)
        for v in range(3):
            value = jnp.where(view == v, cam_ref[v, i], value)
        out.append(value)
    return out


def spread_params(gp):
    odd = iota((8, 128), 0) % 2
    return [
        jnp.where(
            odd == 0,
            jnp.broadcast_to(gp[i : i + 1, 0:128], (8, 128)),
            jnp.broadcast_to(gp[i : i + 1, 128:256], (8, 128)),
        )
        for i in range(59)
    ]


def index_rows(idx_ref, raw_ref, order_ref):
    lane = iota((128, 128), 1)
    first = jnp.broadcast_to(idx_ref[:, 0:1], (128, 128))
    second = jnp.broadcast_to(idx_ref[:, 1:2], (128, 128))
    raw_ref[...] = jnp.where(lane == 0, first, second).astype(F32)
    for q in range(8):
        order_ref[q * 16 : (q + 1) * 16, :] = raw_ref[pl.ds((q // 2) * 32 + q % 2, 16, stride=2), :]


def wait_bytes(ref, count, sem):
    block = ref.at[pl.ds(0, count)]
    pltpu.make_async_copy(block, block, sem).wait()


def step_kernel(
    height, columns,
    har_ref, cen_ref, lsc_ref, rot_ref, opa_ref, cam_ref, idx_ref, list_ref, cnt_ref, target_ref,
    rend_ref, depth_ref, gp_ref, grad_ref,
    raw_idx, ord_idx, small, par3, onehot, feat, sq, send1, recv1, send2, recv2, pick, pick_t, expand, fold,
    halo_x, halo_y, raws, trans, weights, dweights, xsplit, acc, image, gimage, fsc,
    back2s, back2r, back1s, back1r, ssem, rsem,
):
    s = lax.axis_index("space")
    y = lax.axis_index("view")
    x = s // 32
    z = (s // 2) % 16
    c = s % 2
    q = x * 2 + c
    up = (s + 127) % 128
    down = (s + 1) % 128

    def place(q2, z2):
        return ((q2 // 2) * 16 + z2) * 2 + q2 % 2

    ring_peers = []
    for e in range(1, 32):
        q2, y2 = (q + e) % 8, (y + e // 8) % 4
        ring_peers.append((y2 * 8 + q2, (place(q2, z), y2)))
    depth_peers = []
    for d in range(1, 16):
        z2 = (z + d) % 16
        depth_peers.append((z2, (place(q, z2), y)))

    barrier = pltpu.get_barrier_semaphore()
    for _, dev in ring_peers + depth_peers + [(0, ((s + 2 * c + 127) % 128, y))]:
        pl.semaphore_signal(barrier, inc=1, device_id=dev, device_id_type=MESH)

    index_rows(idx_ref, raw_idx, ord_idx)
    idx_t = jnp.transpose(ord_idx[...])
    small[...] = jnp.zeros_like(small)
    small[0:3, :] = cen_ref[...]
    small[3:6, :] = lsc_ref[...]
    small[6:10, :] = rot_ref[...]
    small[10:11, :] = opa_ref[...]

    def gather_chunk(i, carry):
        at = pl.ds(pl.multiple_of(i * 256, 256), 256)
        parts = split(jnp.concatenate([har_ref[:, at], small[:, at]], axis=0), 3)
        for n in range(3):
            par3[n * 64 : (n + 1) * 64, at] = parts[n]
        rows = iota((256, 128), 0).astype(F32) + (i * 256).astype(F32)
        onehot[at, 0:128] = one_hot(rows == idx_t[0:1, :])
        onehot[at, 128:256] = one_hot(rows == idx_t[1:2, :])
        return carry

    lax.fori_loop(0, 16, gather_chunk, 0)
    picked = dot(par3[...], onehot[...])
    gp = picked[0:64] + picked[64:128] + picked[128:192]
    gp_ref[...] = gp
    prm = spread_params(gp)
    features = project(
        prm[0:48], prm[48:51], prm[51:54], prm[54:58], prm[58], view_camera(cam_ref), height, columns
    )
    feat[...] = jnp.zeros_like(feat)
    for f in range(10):
        feat[pl.ds(f, 8, stride=16), :] = features[f]
    sq[...] = jnp.transpose(feat[...])
    quarter = iota((8, 128), 1) // 32
    for a in range(4):
        rows = [sq[pl.ds(a * 32 + z4, 8, stride=4), :] for z4 in range(4)]
        for v in range(4):
            out = rows[v]
            for z4 in range(4):
                if z4 != v:
                    out = jnp.where(quarter == z4, pltpu.roll(rows[z4], ((z4 - v) * 32) % 128, axis=1), out)
            send1[v * 8 + 2 * a] = out[0:4]
            send1[v * 8 + 2 * a + 1] = out[4:8]

    pl.semaphore_wait(barrier, 47)

    def send(src, src_at, dst, dst_at, stage, dev):
        pltpu.make_async_remote_copy(
            src_ref=src.at[src_at], dst_ref=dst.at[dst_at], send_sem=ssem.at[stage], recv_sem=rsem.at[stage],
            device_id=dev, device_id_type=MESH,
        ).start()

    me = y * 8 + q
    for at, dev in ring_peers:
        send(send1, at, recv1, me, 0, dev)
    recv1[me] = send1[me]
    for n in range(3):
        send(target_ref, n, halo_y, n, 1, (down, y))
        send(target_ref, n, halo_y, 3 + n, 1, (up, y))

    tl = list_ref[...].astype(F32)
    prow = iota((128, 1), 0)
    label = (((prow % 8) // 2) * 16 + prow // 8) * 4 + (prow % 2) * 2
    for wj in range(8):
        rows = jnp.broadcast_to((label + (wj // 2) * 256 + wj % 2).astype(F32), (128, 128))
        for t in range(8):
            pick[wj * 128 : (wj + 1) * 128, t * 128 : (t + 1) * 128] = one_hot(rows == tl[t : t + 1, :])
    wait_bytes(recv1, 31, rsem.at[0])
    for zq in range(4):
        rows = [recv1[w * 8 : (w + 1) * 8, zq, :] for w in range(4)]
        for z4 in range(4):
            out = rows[z4]
            for w in range(4):
                if w != z4:
                    out = jnp.where(quarter == w, pltpu.roll(rows[w], ((w - z4) * 32) % 128, axis=1), out)
            send2[zq * 4 + z4] = out

    for at, dev in depth_peers:
        send(send2, at, recv2, z, 2, dev)
    recv2[z] = send2[z]

    pcol = iota((1, 128), 1)
    label = (((pcol % 8) // 2) * 16 + pcol // 8) * 4 + (pcol % 2) * 2
    tl_t = jnp.transpose(jnp.concatenate([tl] * 16, axis=0))
    for t in range(8):
        rows = jnp.broadcast_to(tl_t[:, t : t + 1], (128, 128))
        for wj in range(8):
            cols = (label + (wj // 2) * 256 + wj % 2).astype(F32)
            pick_t[t * 128 : (t + 1) * 128, wj * 128 : (wj + 1) * 128] = one_hot(rows == cols)
    row16 = iota((128, 128), 0)
    lane16 = iota((128, 128), 1)
    for f in range(10):
        grow = one_hot(row16 == (lane16 // 16) * 16 + f)
        for n in range(3):
            expand[n * 128 : (n + 1) * 128, f * 128 : (f + 1) * 128] = grow
        if f < 9:
            shrink = one_hot(lane16 == (row16 // 16) * 16 + f)
            for n in range(2):
                fold[f, n * 128 : (n + 1) * 128, :] = shrink
    lower = one_hot(lane16 < row16)
    upper = one_hot(lane16 > row16)
    lower = jnp.concatenate([lower, lower], axis=1)
    upper = jnp.concatenate([upper, upper], axis=1)
    across = jnp.zeros((128, 128), F32)
    down_rows = iota((32, 48), 1) - iota((32, 48), 0) - 3
    down_band = jnp.zeros((32, 48), F32)
    back_rows = iota((16, 32), 0) + 13 - iota((16, 32), 1)
    back_band = jnp.zeros((16, 32), F32)
    for n in range(11):
        across = jnp.where(row16 - lane16 + 5 == n, WINDOW_TAPS[n], across)
        down_band = jnp.where(down_rows == n, WINDOW_TAPS[n], down_band)
        back_band = jnp.where(back_rows == n, WINDOW_TAPS[n], back_band)

    def blur(images):
        tall = dot_exact(down_band, jnp.concatenate(images, axis=1))
        n = len(images)
        flat = jnp.concatenate([tall[:, i * 128 : (i + 1) * 128] for i in range(n)], axis=0)
        flat = dot_exact(flat, across)
        return [flat[i * 32 : (i + 1) * 32] for i in range(n)]

    def with_halo(halo, n, own):
        above = jnp.where(s > 0, halo[n], 0.0)
        below = jnp.where(s < 127, halo[3 + n], 0.0)
        return jnp.concatenate([above, own, below], axis=0)

    wait_bytes(halo_y, 6, rsem.at[1])
    ys = [with_halo(halo_y, n, target_ref[n]) for n in range(3)]
    y_stats = blur(ys + [v * v for v in ys])
    live = jnp.full((128, 128), cnt_ref[0, 7], jnp.int32)
    for t in range(7):
        live = jnp.where(lane16 // 16 == t, cnt_ref[0, t], live)
    live = row16 < live

    wait_bytes(recv2, 15, rsem.at[2])

    rt = jnp.transpose(recv2[...].reshape(128, 128))
    flat = jnp.concatenate([rt[n * 16 : (n + 1) * 16] for n in range(8)], axis=1)
    got = dot(jnp.concatenate(split(flat, 3), axis=0), pick[...])
    got = got[0:16] + got[16:32] + got[32:48]
    stack = jnp.concatenate([got[:, t * 128 : (t + 1) * 128] for t in range(8)], axis=0)
    listed = jnp.transpose(stack)
    wide = dot(jnp.concatenate(split(listed, 3), axis=1), expand[...])
    dx = wide[:, 0:128] - (lane16.astype(F32) + 0.5)
    ca, cb, cc, op = (wide[:, f * 128 : (f + 1) * 128] for f in range(2, 6))
    fsc[0] = wide[:, 128:256]
    fsc[1] = jnp.where(live, -0.5 * ca * dx * dx, -1e30)
    fsc[2] = cb * dx
    fsc[3] = 0.5 * cc
    fsc[4] = op
    for f in range(4):
        fsc[5 + f] = wide[:, (6 + f) * 128 : (7 + f) * 128]
    fsc[9] = ca * dx
    fsc[10] = cb
    fsc[11] = dx
    first_row = (s * TILE).astype(F32) + 0.5

    def alpha_rows(i, carry):
        at = pl.ds(pl.multiple_of(i * 16, 16), 16)
        low = pl.ds(pl.multiple_of(i * 16 + 128, 16), 16)
        r, ax, bx, c2, o = (fsc[n, at, :] for n in range(5))
        for row in range(16):
            dy = r - (first_row + float(row))
            raw = o * jnp.exp(ax - dy * (bx + c2 * dy))
            raws[row, at, :] = raw
            keep = jnp.log(1.0 - jnp.minimum(raw, ALPHA_MAX))
            high, rest = split(keep, 2)
            xsplit[at, row * 128 : (row + 1) * 128] = high
            xsplit[low, row * 128 : (row + 1) * 128] = rest
        return carry

    lax.fori_loop(0, 8, alpha_rows, 0)

    def compose_row(row, carry):
        lanes = pl.ds(pl.multiple_of(row * 128, 128), 128)
        t = jnp.exp(dot(lower, xsplit[:, lanes]))
        w = jnp.minimum(raws[row], ALPHA_MAX) * t
        trans[row] = t
        weights[row] = w
        for f in range(4):
            image[f, pl.ds(row, 1), :] = jnp.sum(w * fsc[5 + f], axis=0, keepdims=True)
        return carry

    lax.fori_loop(0, 16, compose_row, 0)

    for n in range(3):
        send(image, n, halo_x, n, 3, (down, y))
        send(image, n, halo_x, 3 + n, 3, (up, y))
    for n in range(3):
        rend_ref[n] = image[n]
    depth_ref[...] = image[3]
    wait_bytes(halo_x, 6, rsem.at[3])
    xs = [with_halo(halo_x, n, image[n]) for n in range(3)]
    x_stats = blur(xs + [v * v for v in xs] + [xs[n] * ys[n] for n in range(3)])
    grow = s * TILE - 8 + iota((32, 128), 0)
    share = jnp.where((grow >= 0) & (grow < height), -STRUCTURE_WEIGHT / (TILE * TILE), 0.0)
    pulls = []
    for n in range(3):
        mx, exx, exy = x_stats[n], x_stats[3 + n], x_stats[6 + n]
        my, eyy = y_stats[n], y_stats[3 + n]
        a1 = 2.0 * mx * my + STABLE_MEAN
        a2 = 2.0 * (exy - mx * my) + STABLE_SPREAD
        b1 = mx * mx + my * my + STABLE_MEAN
        b2 = (exx - mx * mx) + (eyy - my * my) + STABLE_SPREAD
        inv = share / (b1 * b2)
        ssim = a1 * a2 / (b1 * b2)
        d_exy = 2.0 * a1 * inv
        d_exx = -ssim * b1 * inv
        d_mx = 2.0 * (my * (a2 - a1) * inv - ssim * mx * (b2 - b1) * inv)
        pulls.append((d_mx, d_exx, d_exy))
    nine = [pulls[n][i] for i in range(3) for n in range(3)]
    tall = dot_exact(back_band, jnp.concatenate(nine, axis=1))
    flat = dot_exact(jnp.concatenate([tall[:, i * 128 : (i + 1) * 128] for i in range(9)], axis=0), across)
    for n in range(3):
        vx, vy = image[n], target_ref[n]
        diff = vx - vy
        smooth = (1.0 - STRUCTURE_WEIGHT) / (TILE * TILE) * diff / jnp.sqrt(diff * diff + SMOOTHING**2)
        b_mx, b_xx, b_xy = (flat[(i * 3 + n) * 16 : (i * 3 + n + 1) * 16] for i in range(3))
        gimage[n] = b_mx + 2.0 * vx * b_xx + vy * b_xy + smooth

    def pull_rows(i, carry):
        at = pl.ds(pl.multiple_of(i * 16, 16), 16)
        low = pl.ds(pl.multiple_of(i * 16 + 128, 16), 16)
        colors = [fsc[5 + f, at, :] for f in range(3)]
        for row in range(16):
            dw = sum(gimage[f, row : row + 1, :] * colors[f] for f in range(3))
            dweights[row, at, :] = dw
            high, rest = split(dw * weights[row, at, :], 2)
            xsplit[at, row * 128 : (row + 1) * 128] = high
            xsplit[low, row * 128 : (row + 1) * 128] = rest
        return carry

    lax.fori_loop(0, 8, pull_rows, 0)

    acc[...] = jnp.zeros_like(acc)

    def pull_alpha(row, carry):
        lanes = pl.ds(pl.multiple_of(row * 128, 128), 128)
        later = dot(upper, xsplit[:, lanes])
        raw = raws[row]
        d_alpha = dweights[row] * trans[row] - later / (1.0 - jnp.minimum(raw, ALPHA_MAX))
        d_power = d_alpha * jnp.where(raw < ALPHA_MAX, raw, jnp.where(raw == ALPHA_MAX, 0.5 * raw, 0.0))
        dy = fsc[0] - (first_row + row.astype(F32))
        moved = d_power * dy
        acc[0] += d_power
        acc[1] += moved
        acc[2] += moved * dy
        w = weights[row]
        for f in range(3):
            acc[3 + f] += w * gimage[f, pl.ds(row, 1), :]
        return carry

    lax.fori_loop(0, 16, pull_alpha, 0)
    s0, s1, s2 = acc[0], acc[1], acc[2]
    adx, cb, dx = fsc[9], fsc[10], fsc[11]
    grads = [
        -(adx * s0 + cb * s1),
        -(2.0 * fsc[3] * s1 + fsc[2] * s0),
        -0.5 * dx * dx * s0,
        -dx * s1,
        -0.5 * s2,
        s0 / fsc[4],
        acc[3],
        acc[4],
        acc[5],
    ]
    folded = sum(dot(jnp.concatenate(split(grads[f], 2), axis=1), fold[f]) for f in range(9))
    turned = jnp.transpose(folded)
    flat = jnp.concatenate([turned[t * 16 : (t + 1) * 16] for t in range(8)], axis=1)
    put = dot(jnp.concatenate(split(flat, 3), axis=0), pick_t[...])
    put = put[0:16] + put[16:32] + put[32:48]
    stack = jnp.concatenate([put[:, n * 128 : (n + 1) * 128] for n in range(8)], axis=0)
    back2s[...] = jnp.transpose(stack).reshape(16, 8, 128)

    for at, dev in depth_peers:
        send(back2s, at, back2r, z, 4, dev)
    back2r[z] = back2s[z]
    wait_bytes(back2r, 15, rsem.at[4])
    for zq in range(4):
        for w in range(4):
            out = back2r[zq * 4 + w]
            for z4 in range(4):
                if z4 != w:
                    moved = pltpu.roll(back2r[zq * 4 + z4], ((z4 - w) * 32) % 128, axis=1)
                    out = jnp.where(quarter == z4, moved, out)
            back1s[w * 8 : (w + 1) * 8, zq, :] = out
    for at, dev in ring_peers:
        send(back1s, at, back1r, me, 5, dev)
    back1r[me] = back1s[me]
    wait_bytes(back1r, 31, rsem.at[5])
    for a in range(4):
        rows = [
            jnp.concatenate([back1r[v * 8 + 2 * a], back1r[v * 8 + 2 * a + 1]], axis=0) for v in range(4)
        ]
        for z4 in range(4):
            out = rows[z4]
            for v in range(4):
                if v != z4:
                    out = jnp.where(quarter == v, pltpu.roll(rows[v], ((v - z4) * 32) % 128, axis=1), out)
            sq[pl.ds(a * 32 + z4, 8, stride=4), :] = out
    grad_ref[...] = jnp.transpose(sq[...])

    wait_bytes(send1, 31, ssem.at[0])
    wait_bytes(halo_y, 6, ssem.at[1])
    wait_bytes(send2, 15, ssem.at[2])
    wait_bytes(halo_x, 6, ssem.at[3])
    wait_bytes(back2s, 15, ssem.at[4])
    wait_bytes(back1s, 31, ssem.at[5])


def owner_kernel(
    height, columns,
    grad_ref, gp_ref, cam_ref, idx_ref,
    har_ref, cen_ref, lsc_ref, rot_ref, opa_ref,
    raw_idx, ord_idx, rows_ref,
):
    prm = spread_params(gp_ref[...])
    cotangents = [grad_ref[pl.ds(f, 8, stride=16), :] for f in range(9)]
    cotangents.append(jnp.zeros((8, 128), F32))
    camera = view_camera(cam_ref)

    def run(harmonics, center, log_scale, quaternion, opacity):
        return project(harmonics, center, log_scale, quaternion, opacity, camera, height, columns)

    _, pull = jax.vjp(run, prm[0:48], prm[48:51], prm[51:54], prm[54:58], prm[58])
    d_har, d_cen, d_lsc, d_rot, d_opa = pull(cotangents)
    rows = list(d_har) + list(d_cen) + list(d_lsc) + list(d_rot) + [d_opa]
    for i in range(59):
        rows_ref[i * 8 : (i + 1) * 8, :] = rows[i]
    for i in range(59, 64):
        rows_ref[i * 8 : (i + 1) * 8, :] = jnp.zeros((8, 128), F32)
    halves = [sum(rows_ref[pl.ds(v * 2 + j, 64, stride=8), :] for v in range(4)) for j in range(2)]
    lhs = jnp.concatenate(split(jnp.concatenate(halves, axis=1), 2), axis=0)
    index_rows(idx_ref, raw_idx, ord_idx)
    first = jnp.broadcast_to(ord_idx[:, 0:1], (128, 256))
    second = jnp.broadcast_to(ord_idx[:, 1:2], (128, 256))

    def put_chunk(i, carry):
        at = pl.ds(pl.multiple_of(i * 256, 256), 256)
        cols = iota((128, 256), 1).astype(F32) + (i * 256).astype(F32)
        hot = jnp.concatenate([one_hot(first == cols), one_hot(second == cols)], axis=0)
        out = dot(lhs, hot)
        out = out[0:64] + out[64:128]
        har_ref[:, at] = out[0:48]
        cen_ref[:, at] = out[48:51]
        lsc_ref[:, at] = out[51:54]
        rot_ref[:, at] = out[54:58]
        opa_ref[:, at] = out[58:59]
        return carry

    lax.fori_loop(0, 16, put_chunk, 0)


def on_device(
    centers, log_scales, rotations, opacity, harmonics, cameras, send_index, tile_lists, counts, target
):
    strips = lax.axis_size("space")
    height = TILE * strips
    columns = target.shape[-1]
    count = centers.shape[1]
    vmem = pl.BlockSpec(memory_space=VMEM)
    smem = pl.BlockSpec(memory_space=pltpu.SMEM)
    index = send_index.reshape(strips, 2)
    dma = pltpu.SemaphoreType.DMA

    def shape(*dims):
        return jax.ShapeDtypeStruct(dims, F32)

    rendered, inverse_depth, gathered, grads = pl.pallas_call(
        functools.partial(step_kernel, height, columns),
        out_shape=[shape(3, 16, 128), shape(16, 128), shape(64, 256), shape(128, 128)],
        in_specs=[vmem] * 5 + [smem, vmem, vmem, smem, vmem],
        out_specs=[vmem] * 4,
        scratch_shapes=[
            VMEM((128, 128), F32),
            VMEM((128, 128), F32),
            VMEM((16, count), F32),
            VMEM((192, count), BF16),
            VMEM((count, 256), BF16),
            VMEM((128, 128), F32),
            VMEM((128, 128), F32),
            VMEM((32, 4, 128), F32),
            VMEM((32, 4, 128), F32),
            VMEM((16, 8, 128), F32),
            VMEM((16, 8, 128), F32),
            VMEM((1024, 1024), BF16),
            VMEM((1024, 1024), BF16),
            VMEM((384, 1280), BF16),
            VMEM((9, 256, 128), BF16),
            VMEM((6, 16, 128), F32),
            VMEM((6, 16, 128), F32),
            VMEM((16, 128, 128), F32),
            VMEM((16, 128, 128), F32),
            VMEM((16, 128, 128), F32),
            VMEM((16, 128, 128), F32),
            VMEM((256, 2048), BF16),
            VMEM((6, 128, 128), F32),
            VMEM((4, 16, 128), F32),
            VMEM((3, 16, 128), F32),
            VMEM((12, 128, 128), F32),
            VMEM((16, 8, 128), F32),
            VMEM((16, 8, 128), F32),
            VMEM((32, 4, 128), F32),
            VMEM((32, 4, 128), F32),
            dma((6,)),
            dma((6,)),
        ],
        compiler_params=pltpu.CompilerParams(
            collective_id=0, has_side_effects=True, vmem_limit_bytes=48 * 2**20
        ),
        name="render_step",
    )(
        harmonics.reshape(48, count),
        centers,
        log_scales,
        rotations,
        opacity.reshape(1, count),
        cameras,
        index,
        tile_lists[0],
        counts,
        target[0],
    )
    d_har, d_cen, d_lsc, d_rot, d_opa = pl.pallas_call(
        functools.partial(owner_kernel, height, columns),
        out_shape=[shape(48, count), shape(3, count), shape(3, count), shape(4, count), shape(1, count)],
        in_specs=[vmem, vmem, smem, vmem],
        out_specs=[vmem] * 5,
        scratch_shapes=[VMEM((128, 128), F32), VMEM((128, 128), F32), VMEM((512, 128), F32)],
        compiler_params=pltpu.CompilerParams(vmem_limit_bytes=32 * 2**20),
        name="owner_pull",
    )(grads, gathered, cameras, index)
    return (
        rendered[None],
        inverse_depth[None],
        d_cen,
        d_lsc,
        d_rot,
        d_opa.reshape(count),
        d_har.reshape(3, 16, count),
    )


def solution(mesh):
    return jax.shard_map(
        on_device,
        mesh=mesh,
        in_specs=(
            P(None, ("space", "view")),
            P(None, ("space", "view")),
            P(None, ("space", "view")),
            P(("space", "view")),
            P(None, None, ("space", "view")),
            P(),
            P("space", "view", None, None),
            P("space", None, None),
            P("space", None),
            P("view", None, "space", None),
        ),
        out_specs=(
            P("view", None, "space", None),
            P("view", "space", None),
            P(None, ("space", "view")),
            P(None, ("space", "view")),
            P(None, ("space", "view")),
            P(("space", "view")),
            P(None, None, ("space", "view")),
        ),
        check_vma=False,
    )
```

```python
import functools
import math

import jax
import jax.numpy as jnp
from jax import lax
from jax.experimental import pallas as pl
from jax.experimental.pallas import tpu as pltpu
from jax.sharding import PartitionSpec as P

TILE = 16
FOCAL_LENGTH = 512.0
LOW_PASS = 0.3
ALPHA_MAX = 0.99
SMOOTHING = 0.05
STRUCTURE_WEIGHT = 0.2
STABLE_MEAN = 0.0001
STABLE_SPREAD = 0.0009
HARMONIC_ZERO = 0.28209479177387814
HARMONIC_ONE = 0.4886025119029199
HARMONIC_TWO = [
    1.0925484305920792,
    -1.0925484305920792,
    0.31539156525252005,
    -1.0925484305920792,
    0.5462742152960396,
]
HARMONIC_THREE = [
    -0.5900435899266435,
    2.890611442640554,
    -0.4570457994644658,
    0.3731763325901154,
    -0.4570457994644658,
    1.445305721320277,
    -0.5900435899266435,
]
TAPS_RAW = [math.exp(-((offset - 5) ** 2) / 4.5) for offset in range(11)]
WINDOW_TAPS = [value / sum(TAPS_RAW) for value in TAPS_RAW]

F32 = jnp.float32
BF16 = jnp.bfloat16
MESH = pl.DeviceIdType.MESH
VMEM = pltpu.VMEM
EXACT = lax.Precision.HIGHEST


def harmonic_basis(ux, uy, uz):
    xx, yy, zz = ux * ux, uy * uy, uz * uz
    return [
        HARMONIC_ZERO * jnp.ones_like(ux),
        -HARMONIC_ONE * uy,
        HARMONIC_ONE * uz,
        -HARMONIC_ONE * ux,
        HARMONIC_TWO[0] * ux * uy,
        HARMONIC_TWO[1] * uy * uz,
        HARMONIC_TWO[2] * (2.0 * zz - xx - yy),
        HARMONIC_TWO[3] * ux * uz,
        HARMONIC_TWO[4] * (xx - yy),
        HARMONIC_THREE[0] * uy * (3.0 * xx - yy),
        HARMONIC_THREE[1] * ux * uy * uz,
        HARMONIC_THREE[2] * uy * (4.0 * zz - xx - yy),
        HARMONIC_THREE[3] * uz * (2.0 * zz - 3.0 * xx - 3.0 * yy),
        HARMONIC_THREE[4] * ux * (4.0 * zz - xx - yy),
        HARMONIC_THREE[5] * uz * (xx - yy),
        HARMONIC_THREE[6] * ux * (xx - 3.0 * yy),
    ]


def geometry(center, log_scale, quaternion, camera, height, columns):
    tx, ty, tz = (center[i] - camera[i] for i in range(3))
    iz = 1.0 / tz
    u = FOCAL_LENGTH * tx * iz + 0.5 * columns
    r = FOCAL_LENGTH * ty * iz + 0.5 * height
    qw, qx, qy, qz = quaternion
    s = 2.0 / (qw * qw + qx * qx + qy * qy + qz * qz)
    rot = [
        [1.0 - s * (qy * qy + qz * qz), s * (qx * qy - qw * qz), s * (qx * qz + qw * qy)],
        [s * (qx * qy + qw * qz), 1.0 - s * (qx * qx + qz * qz), s * (qy * qz - qw * qx)],
        [s * (qx * qz - qw * qy), s * (qy * qz + qw * qx), 1.0 - s * (qx * qx + qy * qy)],
    ]
    scales = [jnp.exp(v) for v in log_scale]
    m = [[rot[i][j] * scales[j] for j in range(3)] for i in range(3)]

    def entry(i, j):
        return m[i][0] * m[j][0] + m[i][1] * m[j][1] + m[i][2] * m[j][2]

    ja = FOCAL_LENGTH * iz
    jx = -FOCAL_LENGTH * tx * iz * iz
    jy = -FOCAL_LENGTH * ty * iz * iz
    sxz, syz, szz = entry(0, 2), entry(1, 2), entry(2, 2)
    pa = ja * ja * entry(0, 0) + 2.0 * ja * jx * sxz + jx * jx * szz + LOW_PASS
    pb = ja * ja * entry(0, 1) + ja * jy * sxz + jx * ja * syz + jx * jy * szz
    pc = ja * ja * entry(1, 1) + 2.0 * ja * jy * syz + jy * jy * szz + LOW_PASS
    det = pa * pc - pb * pb
    return u, r, pc / det, -pb / det, pa / det, iz


def directions(center, camera):
    tx, ty, tz = (center[i] - camera[i] for i in range(3))
    length = jnp.sqrt(tx * tx + ty * ty + tz * tz)
    return harmonic_basis(tx / length, ty / length, tz / length)


def raw_color(harmonics, basis, channel):
    total = harmonics[channel * 16] * basis[0]
    for i in range(1, 16):
        total = total + harmonics[channel * 16 + i] * basis[i]
    return 0.5 + total


def iota(shape, dim):
    return lax.broadcasted_iota(jnp.int32, shape, dim)


def one_hot(condition):
    return jnp.where(condition, 1.0, 0.0).astype(BF16)


def split(value, parts):
    out = []
    for _ in range(parts - 1):
        high = value.astype(BF16)
        out.append(high)
        value = value - high.astype(F32)
    out.append(value.astype(BF16))
    return out


def dot(a, b):
    return jnp.dot(a, b, preferred_element_type=F32)


def dot_exact(a, b):
    return jnp.dot(a, b, preferred_element_type=F32, precision=EXACT)


def take_lanes(values, lanes):
    return jnp.take_along_axis(values, lanes, axis=1, mode="promise_in_bounds")


def view_camera(cam_ref):
    view = iota((8, 128), 0) // 2
    out = []
    for i in range(3):
        value = jnp.broadcast_to(cam_ref[3:4, i : i + 1], (8, 128))
        for v in range(3):
            value = jnp.where(view == v, cam_ref[v : v + 1, i : i + 1], value)
        out.append(value)
    return out


def spread_params(first, second):
    even = iota((8, 128), 0) % 2 == 0
    return [
        jnp.where(
            even,
            jnp.broadcast_to(first[i : i + 1], (8, 128)),
            jnp.broadcast_to(second[i : i + 1], (8, 128)),
        )
        for i in range(59)
    ]


def wait_bytes(ref, count, sem):
    block = ref.at[pl.ds(0, count)]
    pltpu.make_async_copy(block, block, sem).wait()


def step_kernel(
    height, columns,
    har_hbm, cen_hbm, lsc_hbm, rot_hbm, opa_hbm, cam_hbm, idx_hbm, list_hbm, cnt_hbm, target_hbm,
    rend_hbm, depth_hbm, jac_hbm, inv_hbm, grad_hbm,
    har_ref, cen_ref, lsc_ref, rot_ref, opa_ref, cam_ref, idx_ref, list_ref, cnt_ref, target_ref,
    small, feat, sq, send1, recv1, send2, recv2, fold,
    halo_x, halo_y, raws, trans, weights, dweights, xsplit, acc, image, gimage, fsc,
    back2s, back2r, back1s, back1r, jac_ref, inv_ref, lsem, ssem, rsem,
):
    s = lax.axis_index("space")
    y = lax.axis_index("view")
    x = s // 32
    z = (s // 2) % 16
    c = s % 2
    q = x * 2 + c
    up = (s + 127) % 128
    down = (s + 1) % 128

    quarter = iota((8, 128), 1) // 32

    def place(q2, z2):
        return ((q2 // 2) * 16 + z2) * 2 + q2 % 2

    ring_peers = []
    for e in range(1, 32):
        q2, y2 = (q + e) % 8, (y + e // 8) % 4
        ring_peers.append((y2 * 8 + q2, (place(q2, z), y2)))
    depth_peers = []
    for d in (8, 7, 9, 6, 10, 5, 11, 4, 12, 3, 13, 2, 14, 1, 15):
        z2 = (z + d) % 16
        depth_peers.append((z2, (place(q, z2), y)))

    barrier = pltpu.get_barrier_semaphore()
    for _, dev in depth_peers + ring_peers + [(0, ((s + 2 * c + 127) % 128, y))]:
        pl.semaphore_signal(barrier, inc=1, device_id=dev, device_id_type=MESH)
    loads = [
        pltpu.make_async_copy(source, place_in, lsem.at[n])
        for n, (source, place_in) in enumerate((
            (idx_hbm, idx_ref), (har_hbm, har_ref), (cen_hbm, cen_ref), (lsc_hbm, lsc_ref), (rot_hbm, rot_ref),
            (opa_hbm, opa_ref), (cam_hbm, cam_ref), (list_hbm, list_ref), (cnt_hbm, cnt_ref), (target_hbm, target_ref),
        ))
    ]
    for load in loads:
        load.start()
    for load in loads:
        load.wait()

    small[...] = jnp.zeros_like(small)
    small[0:3, :] = cen_ref[...]
    small[3:6, :] = lsc_ref[...]
    small[6:10, :] = rot_ref[...]
    small[10:11, :] = opa_ref[...]
    number = idx_ref[...]
    chunk_of = [jnp.broadcast_to(number[j : j + 1] // 128, (64, 128)) for j in range(2)]
    lane_of = [jnp.broadcast_to(number[j : j + 1] % 128, (64, 128)) for j in range(2)]

    def gather_chunk(i, carry):
        at = pl.ds(pl.multiple_of(i * 128, 128), 128)
        block = jnp.concatenate([har_ref[:, at], small[:, at]], axis=0)
        return tuple(jnp.where(chunk_of[j] == i, take_lanes(block, lane_of[j]), carry[j]) for j in range(2))

    zero = jnp.zeros((64, 128), F32)
    picked = lax.fori_loop(0, har_ref.shape[1] // 128, gather_chunk, (zero, zero), unroll=4)
    prm = spread_params(*picked)
    camera = view_camera(cam_ref)
    center, log_scale, quaternion = prm[48:51], prm[51:54], prm[54:58]
    u, r, ca, cb, cc, iz = geometry(center, log_scale, quaternion, camera, height, columns)
    opaque = 1.0 / (1.0 + jnp.exp(-prm[58]))
    basis = directions(center, camera)
    raw_colors = [raw_color(prm, basis, ch) for ch in range(3)]
    features = [u, r, ca, cb, cc, opaque] + [jnp.maximum(0.0, v) for v in raw_colors] + [iz]
    feat[...] = jnp.zeros_like(feat)
    for f in range(10):
        feat[pl.ds(f, 8, stride=16), :] = features[f]
    sq[...] = jnp.transpose(feat[...])
    for a in range(8):
        first = (a // 2) * 32 + a % 2
        rows = [sq[pl.ds(first + z4 * 2, 4, stride=8), :] for z4 in range(4)]
        for v in range(4):
            out = rows[v]
            for z4 in range(4):
                if z4 != v:
                    moved = pltpu.roll(rows[z4], ((z4 - v) * 32) % 128, axis=1)
                    out = jnp.where(quarter[0:4] == z4, moved, out)
            send1[v * 8 + a] = out

    pl.semaphore_wait(barrier, 47)

    def send(src, src_at, dst, dst_at, stage, dev):
        pltpu.make_async_remote_copy(
            src_ref=src.at[src_at], dst_ref=dst.at[dst_at], send_sem=ssem.at[stage], recv_sem=rsem.at[stage],
            device_id=dev, device_id_type=MESH,
        ).start()

    me = y * 8 + q
    for at, dev in ring_peers:
        send(send1, at, recv1, me, 0, dev)
    recv1[me] = send1[me]
    for n in range(3):
        send(target_ref, n, halo_y, n, 1, (down, y))
        send(target_ref, n, halo_y, 3 + n, 1, (up, y))

    _, pull = jax.vjp(
        lambda *a: geometry(*a, camera, height, columns)[2:5], center, log_scale, quaternion
    )
    one, none = jnp.ones((8, 128), F32), jnp.zeros((8, 128), F32)
    jac = []
    for i in range(3):
        d_center, d_scale, d_turn = pull(tuple(one if i == n else none for n in range(3)))
        jac += list(d_center) + list(d_scale) + list(d_turn)
    passed = [jnp.where(v > 0.0, 1.0, jnp.where(v == 0.0, 0.5, 0.0)) for v in raw_colors]
    for ch in range(3):
        _, pull = jax.vjp(lambda a: raw_color(prm, directions(a, camera), ch), center)
        jac += [passed[ch] * v for v in pull(one)[0]]
    shift = [center[i] - camera[i] for i in range(2)]
    jac += [FOCAL_LENGTH * iz] + [-FOCAL_LENGTH * v * iz * iz for v in shift]
    jac += [opaque * (1.0 - opaque)] + passed + basis
    for n, value in enumerate(jac):
        jac_ref[n] = value

    row128 = iota((128, 128), 0)
    lane128 = iota((128, 128), 1)
    columns_of = jnp.transpose(jnp.concatenate([number.astype(F32)] * 64, axis=0)).astype(jnp.int32)
    total = jnp.zeros((32, 128), F32)
    for j in range(2):
        hit = chunk_of[j][0:32] == iota((32, 128), 0)
        value = jnp.where(hit, (iota((32, 128), 1) + (1 + j * 128)).astype(F32), 0.0).astype(BF16)
        total = total + dot(value, one_hot(columns_of[:, j : j + 1] % 128 == lane128))
    inv_ref[...] = total.astype(jnp.int32)
    stores = [
        pltpu.make_async_copy(jac_ref, jac_hbm, lsem.at[10]),
        pltpu.make_async_copy(inv_ref, inv_hbm, lsem.at[11]),
        pltpu.make_async_copy(image.at[pl.ds(0, 3)], rend_hbm, lsem.at[12]),
        pltpu.make_async_copy(image.at[3], depth_hbm, lsem.at[13]),
        pltpu.make_async_copy(sq, grad_hbm, lsem.at[14]),
    ]
    stores[0].start()
    stores[1].start()

    slot = list_ref[...]
    block_of = (slot // 256) * 2 + slot % 2
    source = (slot // 2) % 128
    lane_in = ((source // 2) % 16) * 8 + (source // 32) * 2 + source % 2
    lane_cols = jnp.transpose(jnp.concatenate([lane_in.astype(F32)] * 16, axis=0)).astype(jnp.int32)
    inverse = jnp.zeros((16, 128), F32)
    for t in range(8):
        hit = jnp.broadcast_to(block_of[t : t + 1], (8, 128)) == iota((8, 128), 0)
        value = jnp.concatenate(
            [jnp.where(hit, float(t), 0.0), jnp.where(hit, iota((8, 128), 1).astype(F32), 0.0)], axis=0
        ).astype(BF16)
        inverse = inverse + dot(value, one_hot(lane_cols[:, t : t + 1] == lane128))
    inverse = inverse.astype(jnp.int32)
    tile_from, entry_from = inverse[0:8], inverse[8:16]
    wait_bytes(recv1, 31, rsem.at[0])
    for zq in range(4):
        rows = [recv1[w * 8 : (w + 1) * 8, zq, :] for w in range(4)]
        for z4 in range(4):
            out = rows[z4]
            for w in range(4):
                if w != z4:
                    out = jnp.where(quarter == w, pltpu.roll(rows[w], ((w - z4) * 32) % 128, axis=1), out)
            send2[zq * 4 + z4] = out

    for at, dev in depth_peers:
        send(send2, at, recv2, z, 2, dev)
    recv2[z] = send2[z]

    row16, lane16 = row128, lane128
    for f in range(9):
        shrink = one_hot(lane16 == (row16 // 16) * 16 + f)
        for n in range(2):
            fold[f, n * 128 : (n + 1) * 128, :] = shrink
    lower = one_hot(lane16 < row16)
    upper = one_hot(lane16 > row16)
    lower = jnp.concatenate([lower, lower], axis=1)
    upper = jnp.concatenate([upper, upper], axis=1)
    across = jnp.zeros((128, 128), F32)
    down_rows = iota((32, 48), 1) - iota((32, 48), 0) - 3
    down_band = jnp.zeros((32, 48), F32)
    back_rows = iota((16, 32), 0) + 13 - iota((16, 32), 1)
    back_band = jnp.zeros((16, 32), F32)
    for n in range(11):
        across = jnp.where(row16 - lane16 + 5 == n, WINDOW_TAPS[n], across)
        down_band = jnp.where(down_rows == n, WINDOW_TAPS[n], down_band)
        back_band = jnp.where(back_rows == n, WINDOW_TAPS[n], back_band)

    def blur(images):
        tall = dot_exact(down_band, jnp.concatenate(images, axis=1))
        n = len(images)
        flat = jnp.concatenate([tall[:, i * 128 : (i + 1) * 128] for i in range(n)], axis=0)
        flat = dot_exact(flat, across)
        return [flat[i * 32 : (i + 1) * 32] for i in range(n)]

    def with_halo(halo, n, own):
        above = jnp.where(s > 0, halo[n], 0.0)
        below = jnp.where(s < 127, halo[3 + n], 0.0)
        return jnp.concatenate([above, own, below], axis=0)

    wait_bytes(halo_y, 6, rsem.at[1])
    ys = [with_halo(halo_y, n, target_ref[n]) for n in range(3)]
    y_stats = blur(ys + [v * v for v in ys])
    live = jnp.broadcast_to(cnt_ref[:, 7:8], (128, 128))
    for t in range(7):
        live = jnp.where(lane16 // 16 == t, cnt_ref[:, t : t + 1], live)
    live = row16 < live

    wait_bytes(recv2, 15, rsem.at[2])

    rt = jnp.transpose(recv2[...].reshape(128, 128))
    tiles = []
    for t in range(8):
        block = jnp.broadcast_to(block_of[t : t + 1], (16, 128))
        lanes = jnp.broadcast_to(lane_in[t : t + 1], (16, 128))
        got = take_lanes(rt[0:16], lanes)
        for n in range(1, 8):
            got = jnp.where(block == n, take_lanes(rt[n * 16 : (n + 1) * 16], lanes), got)
        tiles.append(got)
    listed = jnp.transpose(jnp.concatenate(tiles, axis=0))
    wide = [take_lanes(listed, (lane16 // 16) * 16 + f) for f in range(10)]
    dx = wide[0] - (lane16.astype(F32) + 0.5)
    ca, cb, cc, op = wide[2:6]
    fsc[0] = wide[1]
    fsc[1] = jnp.where(live, -0.5 * ca * dx * dx, -1e30)
    fsc[2] = cb * dx
    fsc[3] = 0.5 * cc
    fsc[4] = op
    for f in range(4):
        fsc[5 + f] = wide[6 + f]
    fsc[9] = ca * dx
    fsc[10] = cb
    fsc[11] = dx
    first_row = (s * TILE).astype(F32) + 0.5

    def alpha_rows(i, carry):
        at = pl.ds(pl.multiple_of(i * 16, 16), 16)
        low = pl.ds(pl.multiple_of(i * 16 + 128, 16), 16)
        r, ax, bx, c2, o = (fsc[n, at, :] for n in range(5))
        for row in range(16):
            dy = r - (first_row + float(row))
            raw = o * jnp.exp(ax - dy * (bx + c2 * dy))
            raws[row, at, :] = raw
            keep = jnp.log(1.0 - jnp.minimum(raw, ALPHA_MAX))
            high, rest = split(keep, 2)
            xsplit[at, row * 128 : (row + 1) * 128] = high
            xsplit[low, row * 128 : (row + 1) * 128] = rest
        return carry

    lax.fori_loop(0, 8, alpha_rows, 0)

    def compose_rows(i, carry):
        lanes = pl.ds(pl.multiple_of(i * 512, 512), 512)
        t4 = jnp.exp(dot(lower, xsplit[:, lanes]))
        for n in range(4):
            row = i * 4 + n
            t = t4[:, n * 128 : (n + 1) * 128]
            w = jnp.minimum(raws[row], ALPHA_MAX) * t
            trans[row] = t
            weights[row] = w
            for f in range(4):
                image[f, pl.ds(row, 1), :] = jnp.sum(w * fsc[5 + f], axis=0, keepdims=True)
        return carry

    lax.fori_loop(0, 4, compose_rows, 0)

    for n in range(3):
        send(image, n, halo_x, n, 3, (down, y))
        send(image, n, halo_x, 3 + n, 3, (up, y))
    stores[2].start()
    stores[3].start()

    def factor_rows(row, carry):
        raw = raws[row]
        moved = jnp.where(raw < ALPHA_MAX, raw, jnp.where(raw == ALPHA_MAX, 0.5 * raw, 0.0))
        raws[row] = moved / (1.0 - jnp.minimum(raw, ALPHA_MAX))
        trans[row] = trans[row] * moved
        return carry

    lax.fori_loop(0, 16, factor_rows, 0)
    wait_bytes(halo_x, 6, rsem.at[3])
    xs = [with_halo(halo_x, n, image[n]) for n in range(3)]
    x_stats = blur(xs + [v * v for v in xs] + [xs[n] * ys[n] for n in range(3)])
    grow = s * TILE - 8 + iota((32, 128), 0)
    share = jnp.where((grow >= 0) & (grow < height), -STRUCTURE_WEIGHT / (TILE * TILE), 0.0)
    pulls = []
    for n in range(3):
        mx, exx, exy = x_stats[n], x_stats[3 + n], x_stats[6 + n]
        my, eyy = y_stats[n], y_stats[3 + n]
        a1 = 2.0 * mx * my + STABLE_MEAN
        a2 = 2.0 * (exy - mx * my) + STABLE_SPREAD
        b1 = mx * mx + my * my + STABLE_MEAN
        b2 = (exx - mx * mx) + (eyy - my * my) + STABLE_SPREAD
        inv = share / (b1 * b2)
        ssim = a1 * a2 / (b1 * b2)
        d_exy = 2.0 * a1 * inv
        d_exx = -ssim * b1 * inv
        d_mx = 2.0 * (my * (a2 - a1) * inv - ssim * mx * (b2 - b1) * inv)
        pulls.append((d_mx, d_exx, d_exy))
    nine = [pulls[n][i] for i in range(3) for n in range(3)]
    tall = dot_exact(back_band, jnp.concatenate(nine, axis=1))
    flat = dot_exact(jnp.concatenate([tall[:, i * 128 : (i + 1) * 128] for i in range(9)], axis=0), across)
    for n in range(3):
        vx, vy = image[n], target_ref[n]
        diff = vx - vy
        smooth = (1.0 - STRUCTURE_WEIGHT) / (TILE * TILE) * diff / jnp.sqrt(diff * diff + SMOOTHING**2)
        b_mx, b_xx, b_xy = (flat[(i * 3 + n) * 16 : (i * 3 + n + 1) * 16] for i in range(3))
        gimage[n] = b_mx + 2.0 * vx * b_xx + vy * b_xy + smooth

    def pull_rows(i, carry):
        at = pl.ds(pl.multiple_of(i * 16, 16), 16)
        low = pl.ds(pl.multiple_of(i * 16 + 128, 16), 16)
        colors = [fsc[5 + f, at, :] for f in range(3)]
        for row in range(16):
            dw = sum(gimage[f, row : row + 1, :] * colors[f] for f in range(3))
            dweights[row, at, :] = dw
            high, rest = split(dw * weights[row, at, :], 2)
            xsplit[at, row * 128 : (row + 1) * 128] = high
            xsplit[low, row * 128 : (row + 1) * 128] = rest
        return carry

    lax.fori_loop(0, 8, pull_rows, 0)

    acc[...] = jnp.zeros_like(acc)

    def pull_alpha(i, carry):
        lanes = pl.ds(pl.multiple_of(i * 512, 512), 512)
        later = dot(upper, xsplit[:, lanes])
        sums = [0.0] * 6
        for n in range(4):
            row = i * 4 + n
            d_power = dweights[row] * trans[row] - later[:, n * 128 : (n + 1) * 128] * raws[row]
            dy = fsc[0] - (first_row + row.astype(F32))
            moved = d_power * dy
            w = weights[row]
            terms = [d_power, moved, moved * dy] + [w * gimage[f, pl.ds(row, 1), :] for f in range(3)]
            sums = [a + b for a, b in zip(sums, terms)]
        for n in range(6):
            acc[n] += sums[n]
        return carry

    lax.fori_loop(0, 4, pull_alpha, 0)
    s0, s1, s2 = acc[0], acc[1], acc[2]
    adx, cb, dx = fsc[9], fsc[10], fsc[11]
    grads = [
        -(adx * s0 + cb * s1),
        -(2.0 * fsc[3] * s1 + fsc[2] * s0),
        -0.5 * dx * dx * s0,
        -dx * s1,
        -0.5 * s2,
        s0 / fsc[4],
        acc[3],
        acc[4],
        acc[5],
    ]
    folded = sum(dot(jnp.concatenate(split(grads[f], 2), axis=1), fold[f]) for f in range(9))
    turned = jnp.transpose(folded)
    blocks = []
    for n in range(8):
        tile = jnp.broadcast_to(tile_from[n : n + 1], (16, 128))
        lanes = jnp.broadcast_to(entry_from[n : n + 1], (16, 128))
        put = take_lanes(turned[0:16], lanes)
        for t in range(1, 8):
            put = jnp.where(tile == t, take_lanes(turned[t * 16 : (t + 1) * 16], lanes), put)
        blocks.append(put)
    back2s[...] = jnp.transpose(jnp.concatenate(blocks, axis=0)).reshape(16, 8, 128)

    for at, dev in depth_peers:
        send(back2s, at, back2r, z, 4, dev)
    back2r[z] = back2s[z]
    wait_bytes(back2r, 15, rsem.at[4])
    for zq in range(4):
        for w in range(4):
            out = back2r[zq * 4 + w]
            for z4 in range(4):
                if z4 != w:
                    moved = pltpu.roll(back2r[zq * 4 + z4], ((z4 - w) * 32) % 128, axis=1)
                    out = jnp.where(quarter == z4, moved, out)
            back1s[w * 8 : (w + 1) * 8, zq, :] = out
    for at, dev in ring_peers:
        send(back1s, at, back1r, me, 5, dev)
    back1r[me] = back1s[me]
    wait_bytes(back1r, 31, rsem.at[5])
    for a in range(8):
        first = (a // 2) * 32 + a % 2
        rows = [back1r[v * 8 + a] for v in range(4)]
        for z4 in range(4):
            out = rows[z4]
            for v in range(4):
                if v != z4:
                    moved = pltpu.roll(rows[v], ((v - z4) * 32) % 128, axis=1)
                    out = jnp.where(quarter[0:4] == v, moved, out)
            sq[pl.ds(first + z4 * 2, 4, stride=8), :] = out
    sq[...] = jnp.transpose(sq[...])
    stores[4].start()

    wait_bytes(send1, 31, ssem.at[0])
    wait_bytes(halo_y, 6, ssem.at[1])
    wait_bytes(send2, 15, ssem.at[2])
    wait_bytes(halo_x, 6, ssem.at[3])
    wait_bytes(back2s, 15, ssem.at[4])
    wait_bytes(back1s, 31, ssem.at[5])
    for store in stores:
        store.wait()


def owner_kernel(
    grad_in, jac_in, inv_in, rend_in, depth_in,
    har_hbm, cen_hbm, lsc_hbm, rot_hbm, opa_hbm, rend_hbm, depth_hbm,
    grad_ref, jac_ref, inv_ref, rows_ref, har_ref, cen_ref, lsc_ref, rot_ref, opa_ref, sem,
):
    loads = [
        pltpu.make_async_copy(grad_in, grad_ref, sem.at[22]),
        pltpu.make_async_copy(jac_in, jac_ref, sem.at[23]),
        pltpu.make_async_copy(inv_in, inv_ref, sem.at[24]),
    ]
    copies = [
        pltpu.make_async_copy(rend_in, rend_hbm, sem.at[0]),
        pltpu.make_async_copy(depth_in, depth_hbm, sem.at[1]),
    ]
    for copy in loads + copies:
        copy.start()
    for load in loads:
        load.wait()
    du, dr, da, db, dc, do, *dcol = [grad_ref[pl.ds(f, 8, stride=16), :] for f in range(9)]
    jac = [jac_ref[n] for n in range(62)]
    conic = (da, db, dc)
    geo = [sum(conic[i] * jac[i * 10 + n] for i in range(3)) for n in range(10)]
    for n in range(3):
        geo[n] = geo[n] + sum(dcol[ch] * jac[30 + ch * 3 + n] for ch in range(3))
    ja, jx, jy, d_opaque = jac[39:43]
    geo[0] = geo[0] + du * ja
    geo[1] = geo[1] + dr * ja
    geo[2] = geo[2] + du * jx + dr * jy
    passed = [dcol[ch] * jac[43 + ch] for ch in range(3)]
    rows = [passed[ch] * jac[46 + i] for ch in range(3) for i in range(16)] + geo + [do * d_opaque]
    for i in range(59):
        rows_ref[i * 8 : (i + 1) * 8, :] = rows[i]
    for i in range(59, 64):
        rows_ref[i * 8 : (i + 1) * 8, :] = jnp.zeros((8, 128), F32)
    halves = [sum(rows_ref[pl.ds(v * 2 + j, 64, stride=8), :] for v in range(4)) for j in range(2)]
    count = har_hbm.shape[1]
    pieces = 4
    wide = count // pieces
    for piece in range(pieces):
        for h in range(piece * wide // 128, (piece + 1) * wide // 128):
            at = slice(h * 128, (h + 1) * 128)
            number = jnp.broadcast_to(inv_ref[h : h + 1, :], (64, 128))
            lanes = (number + 127) % 128
            out = jnp.where(number > 128, take_lanes(halves[1], lanes), take_lanes(halves[0], lanes))
            out = jnp.where(number > 0, out, 0.0)
            har_ref[:, at] = out[0:48]
            cen_ref[:, at] = out[48:51]
            lsc_ref[:, at] = out[51:54]
            rot_ref[:, at] = out[54:58]
            opa_ref[:, at] = out[58:59]
        part = pl.ds(piece * wide, wide)
        for n, (source, target) in enumerate((
            (har_ref, har_hbm), (cen_ref, cen_hbm), (lsc_ref, lsc_hbm), (rot_ref, rot_hbm), (opa_ref, opa_hbm)
        )):
            copy = pltpu.make_async_copy(source.at[:, part], target.at[:, part], sem.at[2 + piece * 5 + n])
            copy.start()
            copies.append(copy)
    for copy in copies:
        copy.wait()


def on_device(
    centers, log_scales, rotations, opacity, harmonics, cameras, send_index, tile_lists, counts, target
):
    strips = lax.axis_size("space")
    height = TILE * strips
    columns = target.shape[-1]
    count = centers.shape[1]
    hbm = pl.BlockSpec(memory_space=pltpu.HBM)
    index = jnp.swapaxes(send_index, 2, 3).reshape(2, strips)
    dma = pltpu.SemaphoreType.DMA

    def shape(*dims):
        return jax.ShapeDtypeStruct(dims, F32)

    params = [VMEM((48, count), F32), VMEM((3, count), F32), VMEM((3, count), F32), VMEM((4, count), F32), VMEM((1, count), F32)]
    rendered, inverse_depth, jacobian, inverse, grads = pl.pallas_call(
        functools.partial(step_kernel, height, columns),
        out_shape=[
            shape(3, 16, 128),
            shape(16, 128),
            shape(62, 8, 128),
            jax.ShapeDtypeStruct((32, 128), jnp.int32),
            shape(128, 128),
        ],
        in_specs=[hbm] * 10,
        out_specs=[hbm] * 5,
        scratch_shapes=params + [
            VMEM((4, 3), F32),
            VMEM((2, 128), jnp.int32),
            VMEM((8, 128), jnp.int32),
            VMEM((1, 8), jnp.int32),
            VMEM((3, 16, 128), F32),
            VMEM((16, count), F32),
            VMEM((128, 128), F32),
            VMEM((128, 128), F32),
            VMEM((32, 4, 128), F32),
            VMEM((32, 4, 128), F32),
            VMEM((16, 8, 128), F32),
            VMEM((16, 8, 128), F32),
            VMEM((9, 256, 128), BF16),
            VMEM((6, 16, 128), F32),
            VMEM((6, 16, 128), F32),
            VMEM((16, 128, 128), F32),
            VMEM((16, 128, 128), F32),
            VMEM((16, 128, 128), F32),
            VMEM((16, 128, 128), F32),
            VMEM((256, 2048), BF16),
            VMEM((6, 128, 128), F32),
            VMEM((4, 16, 128), F32),
            VMEM((3, 16, 128), F32),
            VMEM((12, 128, 128), F32),
            VMEM((16, 8, 128), F32),
            VMEM((16, 8, 128), F32),
            VMEM((32, 4, 128), F32),
            VMEM((32, 4, 128), F32),
            VMEM((62, 8, 128), F32),
            VMEM((32, 128), jnp.int32),
            dma((15,)),
            dma((6,)),
            dma((6,)),
        ],
        compiler_params=pltpu.CompilerParams(
            collective_id=0, has_side_effects=True, vmem_limit_bytes=60 * 2**20
        ),
        name="render_step",
    )(
        harmonics.reshape(48, count),
        centers,
        log_scales,
        rotations,
        opacity.reshape(1, count),
        cameras,
        index,
        tile_lists[0],
        counts,
        target[0],
    )
    d_har, d_cen, d_lsc, d_rot, d_opa, rendered, inverse_depth = pl.pallas_call(
        owner_kernel,
        out_shape=[
            shape(48, count), shape(3, count), shape(3, count), shape(4, count), shape(1, count),
            shape(3, 16, 128), shape(16, 128),
        ],
        in_specs=[hbm] * 5,
        out_specs=[hbm] * 7,
        scratch_shapes=[
            VMEM((128, 128), F32),
            VMEM((62, 8, 128), F32),
            VMEM((32, 128), jnp.int32),
            VMEM((512, 128), F32),
        ]
        + params
        + [dma((25,))],
        compiler_params=pltpu.CompilerParams(vmem_limit_bytes=60 * 2**20),
        name="owner_pull",
    )(grads, jacobian, inverse, rendered, inverse_depth)
    return (
        rendered[None],
        inverse_depth[None],
        d_cen,
        d_lsc,
        d_rot,
        d_opa.reshape(count),
        d_har.reshape(3, 16, count),
    )


def solution(mesh):
    return jax.shard_map(
        on_device,
        mesh=mesh,
        in_specs=(
            P(None, ("space", "view")),
            P(None, ("space", "view")),
            P(None, ("space", "view")),
            P(("space", "view")),
            P(None, None, ("space", "view")),
            P(),
            P("space", "view", None, None),
            P("space", None, None),
            P("space", None),
            P("view", None, "space", None),
        ),
        out_specs=(
            P("view", None, "space", None),
            P("view", "space", None),
            P(None, ("space", "view")),
            P(None, ("space", "view")),
            P(None, ("space", "view")),
            P(("space", "view")),
            P(None, None, ("space", "view")),
        ),
        check_vma=False,
    )
```

```python
import functools
import math

import jax
import jax.numpy as jnp
from jax import lax
from jax.experimental import pallas as pl
from jax.experimental.pallas import tpu as pltpu
from jax.sharding import PartitionSpec as P

TILE = 16
FOCAL_LENGTH = 512.0
LOW_PASS = 0.3
ALPHA_MAX = 0.99
SMOOTHING = 0.05
STRUCTURE_WEIGHT = 0.2
STABLE_MEAN = 0.0001
STABLE_SPREAD = 0.0009
HARMONIC_ZERO = 0.28209479177387814
HARMONIC_ONE = 0.4886025119029199
HARMONIC_TWO = [
    1.0925484305920792,
    -1.0925484305920792,
    0.31539156525252005,
    -1.0925484305920792,
    0.5462742152960396,
]
HARMONIC_THREE = [
    -0.5900435899266435,
    2.890611442640554,
    -0.4570457994644658,
    0.3731763325901154,
    -0.4570457994644658,
    1.445305721320277,
    -0.5900435899266435,
]
TAPS_RAW = [math.exp(-((offset - 5) ** 2) / 4.5) for offset in range(11)]
WINDOW_TAPS = [value / sum(TAPS_RAW) for value in TAPS_RAW]

F32 = jnp.float32
BF16 = jnp.bfloat16
MESH = pl.DeviceIdType.MESH
VMEM = pltpu.VMEM
EXACT = lax.Precision.HIGHEST

SEAT = [0, 1, 2, 3, 4, 8, 9, 10, 11, 12]


def harmonic_basis(ux, uy, uz):
    xx, yy, zz = ux * ux, uy * uy, uz * uz
    return [
        HARMONIC_ZERO * jnp.ones_like(ux),
        -HARMONIC_ONE * uy,
        HARMONIC_ONE * uz,
        -HARMONIC_ONE * ux,
        HARMONIC_TWO[0] * ux * uy,
        HARMONIC_TWO[1] * uy * uz,
        HARMONIC_TWO[2] * (2.0 * zz - xx - yy),
        HARMONIC_TWO[3] * ux * uz,
        HARMONIC_TWO[4] * (xx - yy),
        HARMONIC_THREE[0] * uy * (3.0 * xx - yy),
        HARMONIC_THREE[1] * ux * uy * uz,
        HARMONIC_THREE[2] * uy * (4.0 * zz - xx - yy),
        HARMONIC_THREE[3] * uz * (2.0 * zz - 3.0 * xx - 3.0 * yy),
        HARMONIC_THREE[4] * ux * (4.0 * zz - xx - yy),
        HARMONIC_THREE[5] * uz * (xx - yy),
        HARMONIC_THREE[6] * ux * (xx - 3.0 * yy),
    ]


def geometry(center, log_scale, quaternion, camera, height, columns):
    tx, ty, tz = (center[i] - camera[i] for i in range(3))
    iz = 1.0 / tz
    u = FOCAL_LENGTH * tx * iz + 0.5 * columns
    r = FOCAL_LENGTH * ty * iz + 0.5 * height
    qw, qx, qy, qz = quaternion
    s = 2.0 / (qw * qw + qx * qx + qy * qy + qz * qz)
    rot = [
        [1.0 - s * (qy * qy + qz * qz), s * (qx * qy - qw * qz), s * (qx * qz + qw * qy)],
        [s * (qx * qy + qw * qz), 1.0 - s * (qx * qx + qz * qz), s * (qy * qz - qw * qx)],
        [s * (qx * qz - qw * qy), s * (qy * qz + qw * qx), 1.0 - s * (qx * qx + qy * qy)],
    ]
    scales = [jnp.exp(v) for v in log_scale]
    m = [[rot[i][j] * scales[j] for j in range(3)] for i in range(3)]

    def entry(i, j):
        return m[i][0] * m[j][0] + m[i][1] * m[j][1] + m[i][2] * m[j][2]

    ja = FOCAL_LENGTH * iz
    jx = -FOCAL_LENGTH * tx * iz * iz
    jy = -FOCAL_LENGTH * ty * iz * iz
    sxz, syz, szz = entry(0, 2), entry(1, 2), entry(2, 2)
    pa = ja * ja * entry(0, 0) + 2.0 * ja * jx * sxz + jx * jx * szz + LOW_PASS
    pb = ja * ja * entry(0, 1) + ja * jy * sxz + jx * ja * syz + jx * jy * szz
    pc = ja * ja * entry(1, 1) + 2.0 * ja * jy * syz + jy * jy * szz + LOW_PASS
    det = pa * pc - pb * pb
    return u, r, pc / det, -pb / det, pa / det, iz


def directions(center, camera):
    tx, ty, tz = (center[i] - camera[i] for i in range(3))
    length = jnp.sqrt(tx * tx + ty * ty + tz * tz)
    return harmonic_basis(tx / length, ty / length, tz / length)


def raw_color(harmonics, basis, channel):
    total = harmonics[channel * 16] * basis[0]
    for i in range(1, 16):
        total = total + harmonics[channel * 16 + i] * basis[i]
    return 0.5 + total


def iota(shape, dim):
    return lax.broadcasted_iota(jnp.int32, shape, dim)


def one_hot(condition):
    return jnp.where(condition, 1.0, 0.0).astype(BF16)


def split(value, parts):
    out = []
    for _ in range(parts - 1):
        high = value.astype(BF16)
        out.append(high)
        value = value - high.astype(F32)
    out.append(value.astype(BF16))
    return out


def dot(a, b):
    return jnp.dot(a, b, preferred_element_type=F32)


def dot_exact(a, b):
    return jnp.dot(a, b, preferred_element_type=F32, precision=EXACT)


def take_lanes(values, lanes):
    return jnp.take_along_axis(values, lanes, axis=1, mode="promise_in_bounds")


def view_camera(cam_ref):
    view = iota((8, 128), 0) // 2
    out = []
    for i in range(3):
        value = jnp.broadcast_to(cam_ref[3:4, i : i + 1], (8, 128))
        for v in range(3):
            value = jnp.where(view == v, cam_ref[v : v + 1, i : i + 1], value)
        out.append(value)
    return out


def spread_params(first, second):
    even = iota((8, 128), 0) % 2 == 0
    return [
        jnp.where(
            even,
            jnp.broadcast_to(first[i : i + 1], (8, 128)),
            jnp.broadcast_to(second[i : i + 1], (8, 128)),
        )
        for i in range(first.shape[0])
    ]


def wait_bytes(ref, count, sem):
    block = ref.at[pl.ds(0, count)]
    pltpu.make_async_copy(block, block, sem).wait()


def step_kernel(
    height, columns,
    har_hbm, cen_hbm, lsc_hbm, rot_hbm, opa_hbm, cam_hbm, idx_hbm, list_hbm, cnt_hbm, target_hbm,
    rend_hbm, depth_hbm, inv_hbm, grad_hbm,
    har_ref, cen_ref, lsc_ref, rot_ref, opa_ref, cam_ref, idx_ref, list_ref, cnt_ref, target_ref,
    small, feat, sq, send1, recv1, send2, recv2, fold,
    halo_x, halo_y, raws, trans, weights, dweights, xsplit, acc, image, gimage, fsc,
    back2s, back2r, back1s, back1r, inv_ref, rows_ref, grad_ref, turn, lsem, ssem, rsem,
):
    s = lax.axis_index("space")
    y = lax.axis_index("view")
    x = lax.div(s, 32)
    z = lax.rem(lax.div(s, 2), 16)
    c = lax.rem(s, 2)
    q = x * 2 + c
    up = lax.rem(s + 127, 128)
    down = lax.rem(s + 1, 128)
    quarter = iota((8, 128), 1) // 32

    ring_peers = []
    xs = [lax.rem(x + d, 4) for d in range(4)]
    ys = [lax.rem(y + d, 4) for d in range(4)]
    for dx, dy in sorted(((a, b) for a in range(4) for b in range(4)), key=lambda d: -(d[0] != 0) - (d[1] != 0) - (d[0] == 2) - (d[1] == 2)):
        for c2 in (1 - c, c):
            if dx or dy or c2 is not c:
                ring_peers.append((ys[dy] * 8 + xs[dx] * 2 + c2, (xs[dx] * 32 + z * 2 + c2, ys[dy])))
    depth_peers = []
    for d in (8, 7, 9, 6, 10, 5, 11, 4, 12, 3, 13, 2, 14, 1, 15):
        z2 = lax.rem(z + d, 16)
        depth_peers.append((z2, (x * 32 + z2 * 2 + c, y)))

    pairs = (
        (har_hbm, har_ref), (idx_hbm, idx_ref), (cen_hbm, cen_ref), (lsc_hbm, lsc_ref), (rot_hbm, rot_ref),
        (opa_hbm, opa_ref), (cam_hbm, cam_ref), (list_hbm, list_ref), (cnt_hbm, cnt_ref), (target_hbm, target_ref),
    )
    loads = [pltpu.make_async_copy(a, b, lsem.at[n]) for n, (a, b) in enumerate(pairs)]
    for load in loads:
        load.start()
    barrier = pltpu.get_barrier_semaphore()
    for _, dev in depth_peers + ring_peers + [(0, (lax.rem(s + 2 * c + 127, 128), y))]:
        pl.semaphore_signal(barrier, inc=1, device_id=dev, device_id_type=MESH)
    feat[...] = jnp.zeros_like(feat)
    small[...] = jnp.zeros_like(small)

    for load in loads[1:7]:
        load.wait()
    small[0:3, :] = cen_ref[...]
    small[3:6, :] = lsc_ref[...]
    small[6:10, :] = rot_ref[...]
    small[10:11, :] = opa_ref[...]
    number = idx_ref[...]
    chunk_of = [jnp.broadcast_to(number[j : j + 1] // 128, (64, 128)) for j in range(2)]
    lane_of = [jnp.broadcast_to(number[j : j + 1] % 128, (64, 128)) for j in range(2)]

    def gather(ref):
        rows = ref.shape[0]

        def gather_chunk(i, carry):
            block = ref[:, pl.ds(pl.multiple_of(i * 128, 128), 128)]
            return tuple(
                jnp.where(chunk_of[j][0:rows] == i, take_lanes(block, lane_of[j][0:rows]), carry[j]) for j in range(2)
            )

        zero = jnp.zeros((rows, 128), F32)
        return spread_params(*lax.fori_loop(0, ref.shape[1] // 128, gather_chunk, (zero, zero), unroll=8))

    prm = gather(small)
    camera = view_camera(cam_ref)
    center, log_scale, quaternion = prm[0:3], prm[3:6], prm[6:10]
    u, r, ca, cb, cc, iz = geometry(center, log_scale, quaternion, camera, height, columns)
    opaque = 1.0 / (1.0 + jnp.exp(-prm[10]))
    basis = directions(center, camera)
    loads[0].wait()
    har = gather(har_ref)
    raw_colors = [raw_color(har, basis, ch) for ch in range(3)]
    features = [u, r, ca, cb, cc, opaque] + [jnp.maximum(0.0, v) for v in raw_colors] + [iz]
    for f in range(10):
        feat[pl.ds(SEAT[f], 8, stride=16), :] = features[f]
    sq[...] = jnp.transpose(feat[...])
    for a in range(8):
        first = (a // 2) * 32 + a % 2
        rows = [sq[pl.ds(first + z4 * 2, 4, stride=8), :] for z4 in range(4)]
        for v in range(4):
            out = rows[v]
            for z4 in range(4):
                if z4 != v:
                    moved = pltpu.roll(rows[z4], ((z4 - v) * 32) % 128, axis=1)
                    out = jnp.where(quarter[0:4] == z4, moved, out)
            send1[v * 8 + a] = out

    for load in loads[7:10]:
        load.wait()
    pl.semaphore_wait(barrier, 47)

    def send(src, src_at, dst, dst_at, stage, dev):
        pltpu.make_async_remote_copy(
            src_ref=src.at[src_at], dst_ref=dst.at[dst_at], send_sem=ssem.at[stage], recv_sem=rsem.at[stage],
            device_id=dev, device_id_type=MESH,
        ).start()

    me = y * 8 + q
    for at, dev in ring_peers:
        send(send1, at, recv1, me, 0, dev)
    recv1[me] = send1[me]
    send(target_ref, pl.ds(0, 3), halo_y, pl.ds(0, 3), 1, (down, y))
    send(target_ref, pl.ds(0, 3), halo_y, pl.ds(3, 3), 1, (up, y))

    row128 = iota((128, 128), 0)
    lane128 = iota((128, 128), 1)
    row16, lane16 = row128, lane128
    slot = list_ref[...]
    source = (slot // 2) % 128
    block_of = (source // 2) % 16
    lane_in = (slot % 2) * 32 + (slot // 256) * 8 + (source // 32) * 2 + source % 2
    lane_cols = jnp.transpose(jnp.concatenate([lane_in.astype(F32)] * 16, axis=0)).astype(jnp.int32)
    inverse = jnp.zeros((32, 128), F32)
    for t in range(8):
        hit = jnp.broadcast_to(block_of[t : t + 1], (16, 128)) == iota((16, 128), 0)
        value = jnp.concatenate(
            [jnp.where(hit, float(t), 0.0), jnp.where(hit, iota((16, 128), 1).astype(F32), 0.0)], axis=0
        ).astype(BF16)
        inverse = inverse + dot(value, one_hot(lane_cols[:, t : t + 1] == lane128 % 64))
    inverse = inverse.astype(jnp.int32)
    tile_from, entry_from = inverse[0:16], inverse[16:32]
    stores = [
        pltpu.make_async_copy(inv_ref, inv_hbm, lsem.at[10]),
        pltpu.make_async_copy(image.at[pl.ds(0, 3)], rend_hbm, lsem.at[11]),
        pltpu.make_async_copy(image.at[3], depth_hbm, lsem.at[12]),
        pltpu.make_async_copy(grad_ref, grad_hbm, lsem.at[13]),
    ]
    wait_bytes(recv1, 31, rsem.at[0])
    for zq in range(4):
        for w in range(4):
            turn[zq * 32 + w * 8 : zq * 32 + w * 8 + 8, :] = recv1[w * 8 : (w + 1) * 8, zq, :]
    flat = jnp.transpose(turn[...])
    for z4 in range(4):
        rows = [flat[z4 * 32 + (n % 2) * 16 + (n // 2) * 8 :][0:8] for n in range(4)]
        for zq in range(4):
            out = rows[zq]
            for n in range(4):
                if n != zq:
                    out = jnp.where(quarter == n, pltpu.roll(rows[n], ((n - zq) * 32) % 128, axis=1), out)
            send2[zq * 4 + z4] = out[0:5]

    for at, dev in depth_peers:
        send(send2, at, recv2, z, 2, dev)
    recv2[z] = send2[z]

    for f in range(9):
        shrink = one_hot(row16 == (lane16 // 16) * 16 + SEAT[f])
        for n in range(2):
            fold[:, (f * 2 + n) * 128 : (f * 2 + n + 1) * 128] = shrink
    lower = one_hot(lane16 < row16)
    upper = one_hot(lane16 > row16)
    lower = jnp.concatenate([lower, lower], axis=1)
    upper = jnp.concatenate([upper, upper], axis=1)
    across = jnp.zeros((128, 128), F32)
    down_rows = iota((32, 48), 1) - iota((32, 48), 0) - 3
    down_band = jnp.zeros((32, 48), F32)
    back_rows = iota((16, 32), 0) + 13 - iota((16, 32), 1)
    back_band = jnp.zeros((16, 32), F32)
    for n in range(11):
        across = jnp.where(row16 - lane16 + 5 == n, WINDOW_TAPS[n], across)
        down_band = jnp.where(down_rows == n, WINDOW_TAPS[n], down_band)
        back_band = jnp.where(back_rows == n, WINDOW_TAPS[n], back_band)

    def blur(images):
        tall = dot_exact(down_band, jnp.concatenate(images, axis=1))
        n = len(images)
        flat = jnp.concatenate([tall[:, i * 128 : (i + 1) * 128] for i in range(n)], axis=0)
        flat = dot_exact(flat, across)
        return [flat[i * 32 : (i + 1) * 32] for i in range(n)]

    def with_halo(halo, n, own):
        above = jnp.where(s > 0, halo[n], 0.0)
        below = jnp.where(s < 127, halo[3 + n], 0.0)
        return jnp.concatenate([above, own, below], axis=0)

    wait_bytes(halo_y, 6, rsem.at[1])
    ys = [with_halo(halo_y, n, target_ref[n]) for n in range(3)]
    y_stats = blur(ys + [v * v for v in ys])
    live = jnp.broadcast_to(cnt_ref[:, 7:8], (128, 128))
    for t in range(7):
        live = jnp.where(lane16 // 16 == t, cnt_ref[:, t : t + 1], live)
    live = row16 < live

    wait_bytes(recv2, 15, rsem.at[2])

    got_z = [jnp.concatenate([recv2[n], jnp.zeros((3, 128), F32)], axis=0) for n in range(16)]
    tiles = []
    for t in range(8):
        block = jnp.broadcast_to(block_of[t : t + 1], (8, 128))
        lanes = jnp.broadcast_to(lane_in[t : t + 1], (8, 128))
        for half in range(2):
            got = take_lanes(got_z[0], lanes + half * 64)
            for n in range(1, 16):
                got = jnp.where(block == n, take_lanes(got_z[n], lanes + half * 64), got)
            tiles.append(got)
    listed = jnp.transpose(jnp.concatenate(tiles, axis=0))
    wide = [take_lanes(listed, (lane16 // 16) * 16 + SEAT[f]) for f in range(10)]
    dx = wide[0] - (lane16.astype(F32) + 0.5)
    ca, cb, cc, op = wide[2:6]
    fsc[0] = wide[1]
    fsc[1] = jnp.where(live, -0.5 * ca * dx * dx, -1e30)
    fsc[2] = cb * dx
    fsc[3] = 0.5 * cc
    fsc[4] = op
    for f in range(4):
        fsc[5 + f] = wide[6 + f]
    fsc[9] = ca * dx
    fsc[10] = cb
    fsc[11] = dx
    first_row = (s * TILE).astype(F32) + 0.5

    for i in range(4):
        keeps = []
        for row in range(i * 4, i * 4 + 4):
            dy = fsc[0] - (first_row + float(row))
            raw = fsc[4] * jnp.exp(fsc[1] - dy * (fsc[2] + fsc[3] * dy))
            raws[row] = raw
            keeps.append(jnp.concatenate(split(jnp.log(1.0 - jnp.minimum(raw, ALPHA_MAX)), 2), axis=0))
        t4 = jnp.exp(dot(lower, jnp.concatenate(keeps, axis=1)))
        for n in range(4):
            row = i * 4 + n
            t = t4[:, n * 128 : (n + 1) * 128]
            w = jnp.minimum(raws[row], ALPHA_MAX) * t
            trans[row] = t
            weights[row] = w
            for f in range(4):
                image[f, row : row + 1, :] = jnp.sum(w * fsc[5 + f], axis=0, keepdims=True)

    send(image, pl.ds(0, 3), halo_x, pl.ds(0, 3), 3, (down, y))
    send(image, pl.ds(0, 3), halo_x, pl.ds(3, 3), 3, (up, y))
    stores[1].start()
    stores[2].start()

    def factor_rows(row, carry):
        raw = raws[row]
        moved = jnp.where(raw < ALPHA_MAX, raw, jnp.where(raw == ALPHA_MAX, 0.5 * raw, 0.0))
        raws[row] = moved / (1.0 - jnp.minimum(raw, ALPHA_MAX))
        trans[row] = trans[row] * moved
        return carry

    lax.fori_loop(0, 16, factor_rows, 0)
    wait_bytes(halo_x, 6, rsem.at[3])
    xs = [with_halo(halo_x, n, image[n]) for n in range(3)]
    x_stats = blur(xs + [v * v for v in xs] + [xs[n] * ys[n] for n in range(3)])
    grow = s * TILE - 8 + iota((32, 128), 0)
    share = jnp.where((grow >= 0) & (grow < height), -STRUCTURE_WEIGHT / (TILE * TILE), 0.0)
    pulls = []
    for n in range(3):
        mx, exx, exy = x_stats[n], x_stats[3 + n], x_stats[6 + n]
        my, eyy = y_stats[n], y_stats[3 + n]
        a1 = 2.0 * mx * my + STABLE_MEAN
        a2 = 2.0 * (exy - mx * my) + STABLE_SPREAD
        b1 = mx * mx + my * my + STABLE_MEAN
        b2 = (exx - mx * mx) + (eyy - my * my) + STABLE_SPREAD
        inv = share / (b1 * b2)
        ssim = a1 * a2 / (b1 * b2)
        d_exy = 2.0 * a1 * inv
        d_exx = -ssim * b1 * inv
        d_mx = 2.0 * (my * (a2 - a1) * inv - ssim * mx * (b2 - b1) * inv)
        pulls.append((d_mx, d_exx, d_exy))
    nine = [pulls[n][i] for i in range(3) for n in range(3)]
    tall = dot_exact(back_band, jnp.concatenate(nine, axis=1))
    flat = dot_exact(jnp.concatenate([tall[:, i * 128 : (i + 1) * 128] for i in range(9)], axis=0), across)
    for n in range(3):
        vx, vy = image[n], target_ref[n]
        diff = vx - vy
        smooth = (1.0 - STRUCTURE_WEIGHT) / (TILE * TILE) * diff / jnp.sqrt(diff * diff + SMOOTHING**2)
        b_mx, b_xx, b_xy = (flat[(i * 3 + n) * 16 : (i * 3 + n + 1) * 16] for i in range(3))
        gimage[n] = b_mx + 2.0 * vx * b_xx + vy * b_xy + smooth

    acc[...] = jnp.zeros_like(acc)
    for i in range(4):
        dws, products = [], []
        for row in range(i * 4, i * 4 + 4):
            dw = sum(gimage[f, row : row + 1, :] * fsc[5 + f] for f in range(3))
            dws.append(dw)
            products.append(jnp.concatenate(split(dw * weights[row], 2), axis=0))
        later = dot(upper, jnp.concatenate(products, axis=1))
        sums = [0.0] * 6
        for n in range(4):
            row = i * 4 + n
            d_power = dws[n] * trans[row] - later[:, n * 128 : (n + 1) * 128] * raws[row]
            moved = d_power * (fsc[0] - (first_row + float(row)))
            dy = fsc[0] - (first_row + float(row))
            terms = [d_power, moved, moved * dy]
            terms += [weights[row] * gimage[f, row : row + 1, :] for f in range(3)]
            sums = [a + b for a, b in zip(sums, terms)]
        for n in range(6):
            acc[n] += sums[n]
    s0, s1, s2 = acc[0], acc[1], acc[2]
    adx, cb, dx = fsc[9], fsc[10], fsc[11]
    grads = [
        -(adx * s0 + cb * s1),
        -(2.0 * fsc[3] * s1 + fsc[2] * s0),
        -0.5 * dx * dx * s0,
        -dx * s1,
        -0.5 * s2,
        s0 / fsc[4],
        acc[3],
        acc[4],
        acc[5],
    ]
    parts = [part for f in range(9) for part in split(grads[f], 2)]
    turned = lax.dot_general(
        fold[...], jnp.concatenate(parts, axis=1), (((1,), (1,)), ((), ())), preferred_element_type=F32
    )
    for n in range(16):
        tile = jnp.broadcast_to(tile_from[n : n + 1], (8, 128))
        lanes = jnp.broadcast_to(entry_from[n : n + 1], (8, 128))
        halves = []
        for half in range(2):
            put = take_lanes(turned[half * 8 : half * 8 + 8], lanes)
            for t in range(1, 8):
                at = t * 16 + half * 8
                put = jnp.where(tile == t, take_lanes(turned[at : at + 8], lanes), put)
            halves.append(put)
        back2s[n] = jnp.where(quarter < 2, halves[0], halves[1])[0:5]

    for at, dev in depth_peers:
        send(back2s, at, back2r, z, 4, dev)
    back2r[z] = back2s[z]
    _, pull = jax.vjp(
        lambda *a: geometry(*a, camera, height, columns)[2:5], center, log_scale, quaternion
    )
    one, none = jnp.ones((8, 128), F32), jnp.zeros((8, 128), F32)
    jac = []
    for i in range(3):
        d_center, d_scale, d_turn = pull(tuple(one if i == n else none for n in range(3)))
        jac += list(d_center) + list(d_scale) + list(d_turn)
    passed = [jnp.where(v > 0.0, 1.0, jnp.where(v == 0.0, 0.5, 0.0)) for v in raw_colors]
    for ch in range(3):
        _, pull = jax.vjp(lambda a: raw_color(har, directions(a, camera), ch), center)
        jac += [passed[ch] * v for v in pull(one)[0]]
    shift = [center[i] - camera[i] for i in range(2)]
    jac += [FOCAL_LENGTH * iz] + [-FOCAL_LENGTH * v * iz * iz for v in shift]
    jac += [opaque * (1.0 - opaque)]

    columns_of = jnp.transpose(jnp.concatenate([number.astype(F32)] * 64, axis=0)).astype(jnp.int32)
    total = jnp.zeros((32, 128), F32)
    for j in range(2):
        hit = chunk_of[j][0:32] == iota((32, 128), 0)
        value = jnp.where(hit, (iota((32, 128), 1) + (1 + j * 128)).astype(F32), 0.0).astype(BF16)
        total = total + dot(value, one_hot(columns_of[:, j : j + 1] % 128 == lane128))
    inv_ref[...] = total.astype(jnp.int32)
    stores[0].start()
    wait_bytes(back2r, 15, rsem.at[4])
    back_z = [jnp.concatenate([back2r[n], jnp.zeros((3, 128), F32)], axis=0) for n in range(16)]
    for z4 in range(4):
        for n in range(4):
            out = back_z[n * 4 + z4]
            for zq in range(4):
                if zq != n:
                    moved = pltpu.roll(back_z[zq * 4 + z4], ((zq - n) * 32) % 128, axis=1)
                    out = jnp.where(quarter == zq, moved, out)
            at = z4 * 32 + (n % 2) * 16 + (n // 2) * 8
            turn[at : at + 8, :] = out
    turn[...] = jnp.transpose(turn[...])
    for zq in range(4):
        for w in range(4):
            back1s[w * 8 : (w + 1) * 8, zq, :] = turn[zq * 32 + w * 8 : zq * 32 + w * 8 + 8, :]
    for at, dev in ring_peers:
        send(back1s, at, back1r, me, 5, dev)
    back1r[me] = back1s[me]
    wait_bytes(back1r, 31, rsem.at[5])
    for a in range(8):
        first = (a // 2) * 32 + a % 2
        rows = [back1r[v * 8 + a] for v in range(4)]
        for z4 in range(4):
            out = rows[z4]
            for v in range(4):
                if v != z4:
                    moved = pltpu.roll(rows[v], ((v - z4) * 32) % 128, axis=1)
                    out = jnp.where(quarter[0:4] == v, moved, out)
            sq[pl.ds(first + z4 * 2, 4, stride=8), :] = out
    turn[...] = jnp.transpose(sq[...])
    du, dr, da, db, dc, do, *dcol = [turn[pl.ds(SEAT[f], 8, stride=16), :] for f in range(9)]
    conic = (da, db, dc)
    geo = [sum(conic[i] * jac[i * 10 + n] for i in range(3)) for n in range(10)]
    for n in range(3):
        geo[n] = geo[n] + sum(dcol[ch] * jac[30 + ch * 3 + n] for ch in range(3))
    ja, jx, jy, d_opaque = jac[39:43]
    geo[0] = geo[0] + du * ja
    geo[1] = geo[1] + dr * ja
    geo[2] = geo[2] + du * jx + dr * jy
    shown = [dcol[ch] * passed[ch] for ch in range(3)]
    rows = [shown[ch] * basis[i] for ch in range(3) for i in range(16)] + geo + [do * d_opaque]
    for i in range(59):
        rows_ref[i * 8 : (i + 1) * 8, :] = rows[i]
    for i in range(59, 64):
        rows_ref[i * 8 : (i + 1) * 8, :] = none
    for j in range(2):
        grad_ref[j] = sum(rows_ref[pl.ds(v * 2 + j, 64, stride=8), :] for v in range(4))
    stores[3].start()

    wait_bytes(send1, 31, ssem.at[0])
    wait_bytes(halo_y, 6, ssem.at[1])
    wait_bytes(send2, 15, ssem.at[2])
    wait_bytes(halo_x, 6, ssem.at[3])
    wait_bytes(back2s, 15, ssem.at[4])
    wait_bytes(back1s, 31, ssem.at[5])
    for store in stores:
        store.wait()


def owner_kernel(
    grad_in, inv_in, rend_in, depth_in,
    har_hbm, cen_hbm, lsc_hbm, rot_hbm, opa_hbm, rend_hbm, depth_hbm,
    grad_ref, inv_ref, har_ref, cen_ref, lsc_ref, rot_ref, opa_ref, sem,
):
    loads = [
        pltpu.make_async_copy(grad_in, grad_ref, sem.at[22]),
        pltpu.make_async_copy(inv_in, inv_ref, sem.at[23]),
    ]
    copies = [
        pltpu.make_async_copy(rend_in, rend_hbm, sem.at[0]),
        pltpu.make_async_copy(depth_in, depth_hbm, sem.at[1]),
    ]
    for copy in loads + copies:
        copy.start()
    for load in loads:
        load.wait()
    halves = [grad_ref[j] for j in range(2)]
    count = har_hbm.shape[1]
    pieces = 4
    wide = count // pieces
    for piece in range(pieces):
        for h in range(piece * wide // 128, (piece + 1) * wide // 128):
            at = slice(h * 128, (h + 1) * 128)
            number = jnp.broadcast_to(inv_ref[h : h + 1, :], (64, 128))
            lanes = (number + 127) % 128
            out = jnp.where(number > 128, take_lanes(halves[1], lanes), take_lanes(halves[0], lanes))
            out = jnp.where(number > 0, out, 0.0)
            har_ref[:, at] = out[0:48]
            cen_ref[:, at] = out[48:51]
            lsc_ref[:, at] = out[51:54]
            rot_ref[:, at] = out[54:58]
            opa_ref[:, at] = out[58:59]
        part = pl.ds(piece * wide, wide)
        for n, (source, target) in enumerate((
            (har_ref, har_hbm), (cen_ref, cen_hbm), (lsc_ref, lsc_hbm), (rot_ref, rot_hbm), (opa_ref, opa_hbm)
        )):
            copy = pltpu.make_async_copy(source.at[:, part], target.at[:, part], sem.at[2 + piece * 5 + n])
            copy.start()
            copies.append(copy)
    for copy in copies:
        copy.wait()


def on_device(
    centers, log_scales, rotations, opacity, harmonics, cameras, send_index, tile_lists, counts, target
):
    strips = lax.axis_size("space")
    height = TILE * strips
    columns = target.shape[-1]
    count = centers.shape[1]
    hbm = pl.BlockSpec(memory_space=pltpu.HBM)
    index = jnp.swapaxes(send_index, 2, 3).reshape(2, strips)
    dma = pltpu.SemaphoreType.DMA

    def shape(*dims):
        return jax.ShapeDtypeStruct(dims, F32)

    params = [VMEM((48, count), F32), VMEM((3, count), F32), VMEM((3, count), F32), VMEM((4, count), F32), VMEM((1, count), F32)]
    rendered, inverse_depth, inverse, grads = pl.pallas_call(
        functools.partial(step_kernel, height, columns),
        out_shape=[
            shape(3, 16, 128),
            shape(16, 128),
            jax.ShapeDtypeStruct((32, 128), jnp.int32),
            shape(2, 64, 128),
        ],
        in_specs=[hbm] * 10,
        out_specs=[hbm] * 4,
        scratch_shapes=params + [
            VMEM((4, 3), F32),
            VMEM((2, 128), jnp.int32),
            VMEM((8, 128), jnp.int32),
            VMEM((1, 8), jnp.int32),
            VMEM((3, 16, 128), F32),
            VMEM((16, count), F32),
            VMEM((128, 128), F32),
            VMEM((128, 128), F32),
            VMEM((32, 4, 128), F32),
            VMEM((32, 4, 128), F32),
            VMEM((16, 5, 128), F32),
            VMEM((16, 5, 128), F32),
            VMEM((128, 2304), BF16),
            VMEM((6, 16, 128), F32),
            VMEM((6, 16, 128), F32),
            VMEM((16, 128, 128), F32),
            VMEM((16, 128, 128), F32),
            VMEM((16, 128, 128), F32),
            VMEM((16, 128, 128), F32),
            VMEM((256, 2048), BF16),
            VMEM((6, 128, 128), F32),
            VMEM((4, 16, 128), F32),
            VMEM((3, 16, 128), F32),
            VMEM((12, 128, 128), F32),
            VMEM((16, 5, 128), F32),
            VMEM((16, 5, 128), F32),
            VMEM((32, 4, 128), F32),
            VMEM((32, 4, 128), F32),
            VMEM((32, 128), jnp.int32),
            VMEM((512, 128), F32),
            VMEM((2, 64, 128), F32),
            VMEM((128, 128), F32),
            dma((14,)),
            dma((6,)),
            dma((6,)),
        ],
        compiler_params=pltpu.CompilerParams(
            collective_id=0, has_side_effects=True, vmem_limit_bytes=60 * 2**20
        ),
        name="render_step",
    )(
        harmonics.reshape(48, count),
        centers,
        log_scales,
        rotations,
        opacity.reshape(1, count),
        cameras,
        index,
        tile_lists[0],
        counts,
        target[0],
    )
    d_har, d_cen, d_lsc, d_rot, d_opa, rendered, inverse_depth = pl.pallas_call(
        owner_kernel,
        out_shape=[
            shape(48, count), shape(3, count), shape(3, count), shape(4, count), shape(1, count),
            shape(3, 16, 128), shape(16, 128),
        ],
        in_specs=[hbm] * 4,
        out_specs=[hbm] * 7,
        scratch_shapes=[
            VMEM((2, 64, 128), F32),
            VMEM((32, 128), jnp.int32),
        ]
        + params
        + [dma((24,))],
        compiler_params=pltpu.CompilerParams(vmem_limit_bytes=60 * 2**20),
        name="owner_pull",
    )(grads, inverse, rendered, inverse_depth)
    return (
        rendered[None],
        inverse_depth[None],
        d_cen,
        d_lsc,
        d_rot,
        d_opa.reshape(count),
        d_har.reshape(3, 16, count),
    )


def solution(mesh):
    return jax.shard_map(
        on_device,
        mesh=mesh,
        in_specs=(
            P(None, ("space", "view")),
            P(None, ("space", "view")),
            P(None, ("space", "view")),
            P(("space", "view")),
            P(None, None, ("space", "view")),
            P(),
            P("space", "view", None, None),
            P("space", None, None),
            P("space", None),
            P("view", None, "space", None),
        ),
        out_specs=(
            P("view", None, "space", None),
            P("view", "space", None),
            P(None, ("space", "view")),
            P(None, ("space", "view")),
            P(None, ("space", "view")),
            P(("space", "view")),
            P(None, None, ("space", "view")),
        ),
        check_vma=False,
    )
```

```python
import functools
import math

import jax
import jax.numpy as jnp
from jax import lax
from jax.experimental import pallas as pl
from jax.experimental.pallas import tpu as pltpu
from jax.sharding import PartitionSpec as P

TILE = 16
FOCAL_LENGTH = 512.0
LOW_PASS = 0.3
ALPHA_MAX = 0.99
SMOOTHING = 0.05
STRUCTURE_WEIGHT = 0.2
STABLE_MEAN = 0.0001
STABLE_SPREAD = 0.0009
HARMONIC_ZERO = 0.28209479177387814
HARMONIC_ONE = 0.4886025119029199
HARMONIC_TWO = [
    1.0925484305920792,
    -1.0925484305920792,
    0.31539156525252005,
    -1.0925484305920792,
    0.5462742152960396,
]
HARMONIC_THREE = [
    -0.5900435899266435,
    2.890611442640554,
    -0.4570457994644658,
    0.3731763325901154,
    -0.4570457994644658,
    1.445305721320277,
    -0.5900435899266435,
]
TAPS_RAW = [math.exp(-((offset - 5) ** 2) / 4.5) for offset in range(11)]
WINDOW_TAPS = [value / sum(TAPS_RAW) for value in TAPS_RAW]

F32 = jnp.float32
BF16 = jnp.bfloat16
MESH = pl.DeviceIdType.MESH
VMEM = pltpu.VMEM
EXACT = lax.Precision.HIGHEST

SEAT = [0, 1, 2, 3, 4, 8, 9, 10, 11, 12]


def harmonic_basis(ux, uy, uz):
    xx, yy, zz = ux * ux, uy * uy, uz * uz
    return [
        HARMONIC_ZERO * jnp.ones_like(ux),
        -HARMONIC_ONE * uy,
        HARMONIC_ONE * uz,
        -HARMONIC_ONE * ux,
        HARMONIC_TWO[0] * ux * uy,
        HARMONIC_TWO[1] * uy * uz,
        HARMONIC_TWO[2] * (2.0 * zz - xx - yy),
        HARMONIC_TWO[3] * ux * uz,
        HARMONIC_TWO[4] * (xx - yy),
        HARMONIC_THREE[0] * uy * (3.0 * xx - yy),
        HARMONIC_THREE[1] * ux * uy * uz,
        HARMONIC_THREE[2] * uy * (4.0 * zz - xx - yy),
        HARMONIC_THREE[3] * uz * (2.0 * zz - 3.0 * xx - 3.0 * yy),
        HARMONIC_THREE[4] * ux * (4.0 * zz - xx - yy),
        HARMONIC_THREE[5] * uz * (xx - yy),
        HARMONIC_THREE[6] * ux * (xx - 3.0 * yy),
    ]


def geometry(center, log_scale, quaternion, camera, height, columns):
    tx, ty, tz = (center[i] - camera[i] for i in range(3))
    iz = 1.0 / tz
    u = FOCAL_LENGTH * tx * iz + 0.5 * columns
    r = FOCAL_LENGTH * ty * iz + 0.5 * height
    qw, qx, qy, qz = quaternion
    s = 2.0 / (qw * qw + qx * qx + qy * qy + qz * qz)
    rot = [
        [1.0 - s * (qy * qy + qz * qz), s * (qx * qy - qw * qz), s * (qx * qz + qw * qy)],
        [s * (qx * qy + qw * qz), 1.0 - s * (qx * qx + qz * qz), s * (qy * qz - qw * qx)],
        [s * (qx * qz - qw * qy), s * (qy * qz + qw * qx), 1.0 - s * (qx * qx + qy * qy)],
    ]
    scales = [jnp.exp(v) for v in log_scale]
    m = [[rot[i][j] * scales[j] for j in range(3)] for i in range(3)]

    def entry(i, j):
        return m[i][0] * m[j][0] + m[i][1] * m[j][1] + m[i][2] * m[j][2]

    ja = FOCAL_LENGTH * iz
    jx = -FOCAL_LENGTH * tx * iz * iz
    jy = -FOCAL_LENGTH * ty * iz * iz
    sxz, syz, szz = entry(0, 2), entry(1, 2), entry(2, 2)
    pa = ja * ja * entry(0, 0) + 2.0 * ja * jx * sxz + jx * jx * szz + LOW_PASS
    pb = ja * ja * entry(0, 1) + ja * jy * sxz + jx * ja * syz + jx * jy * szz
    pc = ja * ja * entry(1, 1) + 2.0 * ja * jy * syz + jy * jy * szz + LOW_PASS
    det = pa * pc - pb * pb
    return u, r, pc / det, -pb / det, pa / det, iz


def directions(center, camera):
    tx, ty, tz = (center[i] - camera[i] for i in range(3))
    length = jnp.sqrt(tx * tx + ty * ty + tz * tz)
    return harmonic_basis(tx / length, ty / length, tz / length)


def raw_color(harmonics, basis, channel):
    total = harmonics[channel * 16] * basis[0]
    for i in range(1, 16):
        total = total + harmonics[channel * 16 + i] * basis[i]
    return 0.5 + total


def iota(shape, dim):
    return lax.broadcasted_iota(jnp.int32, shape, dim)


def one_hot(condition):
    return jnp.where(condition, 1.0, 0.0).astype(BF16)


def split(value, parts):
    out = []
    for _ in range(parts - 1):
        high = value.astype(BF16)
        out.append(high)
        value = value - high.astype(F32)
    out.append(value.astype(BF16))
    return out


def dot(a, b):
    return jnp.dot(a, b, preferred_element_type=F32)


def dot_exact(a, b):
    return jnp.dot(a, b, preferred_element_type=F32, precision=EXACT)


def take_lanes(values, lanes):
    return jnp.take_along_axis(values, lanes, axis=1, mode="promise_in_bounds")


def view_camera(cam_ref):
    view = iota((8, 128), 0) // 2
    out = []
    for i in range(3):
        value = jnp.broadcast_to(cam_ref[3:4, i : i + 1], (8, 128))
        for v in range(3):
            value = jnp.where(view == v, cam_ref[v : v + 1, i : i + 1], value)
        out.append(value)
    return out


def spread_params(first, second):
    even = iota((8, 128), 0) % 2 == 0
    return [
        jnp.where(
            even,
            jnp.broadcast_to(first[i : i + 1], (8, 128)),
            jnp.broadcast_to(second[i : i + 1], (8, 128)),
        )
        for i in range(first.shape[0])
    ]


def wait_bytes(ref, count, sem):
    block = ref.at[pl.ds(0, count)]
    pltpu.make_async_copy(block, block, sem).wait()


def step_kernel(
    height, columns,
    har_hbm, cen_hbm, lsc_hbm, rot_hbm, opa_hbm, cam_hbm, idx_hbm, list_hbm, cnt_hbm, target_hbm,
    rend_hbm, depth_hbm, inv_hbm, grad_hbm,
    har_ref, cen_ref, lsc_ref, rot_ref, opa_ref, cam_ref, idx_ref, list_ref, cnt_ref, target_ref,
    small, feat, sq, send1, recv1, send2, recv2, fold,
    halo_x, halo_y, raws, trans, weights, dweights, xsplit, image, gimage, fsc,
    back2s, back2r, back1s, back1r, inv_ref, rows_ref, grad_ref, turn, lsem, ssem, rsem,
):
    s = lax.axis_index("space")
    y = lax.axis_index("view")
    x = lax.div(s, 32)
    z = lax.rem(lax.div(s, 2), 16)
    c = lax.rem(s, 2)
    q = x * 2 + c
    up = lax.rem(s + 127, 128)
    down = lax.rem(s + 1, 128)
    quarter = iota((8, 128), 1) // 32

    ring_peers = []
    xs = [lax.rem(x + d, 4) for d in range(4)]
    ys = [lax.rem(y + d, 4) for d in range(4)]
    for dx, dy in sorted(((a, b) for a in range(4) for b in range(4)), key=lambda d: -(d[0] != 0) - (d[1] != 0) - (d[0] == 2) - (d[1] == 2)):
        for c2 in (1 - c, c):
            if dx or dy or c2 is not c:
                ring_peers.append((ys[dy] * 8 + xs[dx] * 2 + c2, (xs[dx] * 32 + z * 2 + c2, ys[dy])))
    depth_peers = []
    for d in (8, 7, 9, 6, 10, 5, 11, 4, 12, 3, 13, 2, 14, 1, 15):
        z2 = lax.rem(z + d, 16)
        depth_peers.append((z2, (x * 32 + z2 * 2 + c, y)))

    barrier = pltpu.get_barrier_semaphore()
    for _, dev in depth_peers:
        pl.semaphore_signal(barrier, inc=1, device_id=dev, device_id_type=MESH)
    pairs = (
        (har_hbm, har_ref), (idx_hbm, idx_ref), (cen_hbm, cen_ref), (lsc_hbm, lsc_ref), (rot_hbm, rot_ref),
        (opa_hbm, opa_ref), (cam_hbm, cam_ref), (list_hbm, list_ref), (cnt_hbm, cnt_ref), (target_hbm, target_ref),
    )
    loads = [pltpu.make_async_copy(a, b, lsem.at[n]) for n, (a, b) in enumerate(pairs)]
    for load in loads:
        load.start()
    for _, dev in ring_peers + [(0, (lax.rem(s + 2 * c + 127, 128), y))]:
        pl.semaphore_signal(barrier, inc=1, device_id=dev, device_id_type=MESH)

    feat[...] = jnp.zeros_like(feat)
    small[...] = jnp.zeros_like(small)

    for load in loads[1:7]:
        load.wait()
    small[0:3, :] = cen_ref[...]
    small[3:6, :] = lsc_ref[...]
    small[6:10, :] = rot_ref[...]
    small[10:11, :] = opa_ref[...]
    number = idx_ref[...]
    chunk_of = [jnp.broadcast_to(number[j : j + 1] // 128, (64, 128)) for j in range(2)]
    lane_of = [jnp.broadcast_to(number[j : j + 1] % 128, (64, 128)) for j in range(2)]

    def gather(ref):
        rows = ref.shape[0]

        def gather_chunk(i, carry):
            block = ref[:, pl.ds(pl.multiple_of(i * 128, 128), 128)]
            return tuple(
                jnp.where(chunk_of[j][0:rows] == i, take_lanes(block, lane_of[j][0:rows]), carry[j]) for j in range(2)
            )

        zero = jnp.zeros((rows, 128), F32)
        return spread_params(*lax.fori_loop(0, ref.shape[1] // 128, gather_chunk, (zero, zero), unroll=8))

    prm = gather(small)
    camera = view_camera(cam_ref)
    center, log_scale, quaternion = prm[0:3], prm[3:6], prm[6:10]
    u, r, ca, cb, cc, iz = geometry(center, log_scale, quaternion, camera, height, columns)
    opaque = 1.0 / (1.0 + jnp.exp(-prm[10]))
    basis = directions(center, camera)
    loads[0].wait()
    har = gather(har_ref)
    raw_colors = [raw_color(har, basis, ch) for ch in range(3)]
    features = [u, r, ca, cb, cc, opaque] + [jnp.maximum(0.0, v) for v in raw_colors] + [iz]
    for f in range(10):
        feat[pl.ds(SEAT[f], 8, stride=16), :] = features[f]
    sq[...] = jnp.transpose(feat[...])
    for a in range(8):
        first = (a // 2) * 32 + a % 2
        rows = [sq[pl.ds(first + z4 * 2, 4, stride=8), :] for z4 in range(4)]
        for v in range(4):
            out = rows[v]
            for z4 in range(4):
                if z4 != v:
                    moved = pltpu.roll(rows[z4], ((z4 - v) * 32) % 128, axis=1)
                    out = jnp.where(quarter[0:4] == z4, moved, out)
            send1[v * 8 + a] = out

    for load in loads[7:10]:
        load.wait()
    pl.semaphore_wait(barrier, 47)

    def send(src, src_at, dst, dst_at, stage, dev):
        pltpu.make_async_remote_copy(
            src_ref=src.at[src_at], dst_ref=dst.at[dst_at], send_sem=ssem.at[stage], recv_sem=rsem.at[stage],
            device_id=dev, device_id_type=MESH,
        ).start()

    me = y * 8 + q
    for at, dev in ring_peers:
        send(send1, at, recv1, me, 0, dev)
    recv1[me] = send1[me]
    send(target_ref, pl.ds(0, 3), halo_y, pl.ds(0, 3), 1, (down, y))
    send(target_ref, pl.ds(0, 3), halo_y, pl.ds(3, 3), 1, (up, y))

    row128 = iota((128, 128), 0)
    lane128 = iota((128, 128), 1)
    row16, lane16 = row128, lane128
    slot = list_ref[...]
    source = (slot // 2) % 128
    block_of = (source // 2) % 16
    lane_in = (slot % 2) * 32 + (slot // 256) * 8 + (source // 32) * 2 + source % 2
    lane_cols = jnp.transpose(jnp.concatenate([lane_in.astype(F32)] * 16, axis=0)).astype(jnp.int32)
    inverse = jnp.zeros((32, 128), F32)
    for t in range(8):
        hit = jnp.broadcast_to(block_of[t : t + 1], (16, 128)) == iota((16, 128), 0)
        value = jnp.concatenate(
            [jnp.where(hit, float(t), 0.0), jnp.where(hit, iota((16, 128), 1).astype(F32), 0.0)], axis=0
        ).astype(BF16)
        inverse = inverse + dot(value, one_hot(lane_cols[:, t : t + 1] == lane128 % 64))
    inverse = inverse.astype(jnp.int32)
    tile_from, entry_from = inverse[0:16], inverse[16:32]
    stores = [
        pltpu.make_async_copy(inv_ref, inv_hbm, lsem.at[10]),
        pltpu.make_async_copy(image.at[pl.ds(0, 3)], rend_hbm, lsem.at[11]),
        pltpu.make_async_copy(image.at[3], depth_hbm, lsem.at[12]),
        pltpu.make_async_copy(grad_ref, grad_hbm, lsem.at[13]),
    ]
    wait_bytes(recv1, 31, rsem.at[0])
    for zq in range(4):
        for w in range(4):
            turn[zq * 32 + w * 8 : zq * 32 + w * 8 + 8, :] = recv1[w * 8 : (w + 1) * 8, zq, :]
    flat = jnp.transpose(turn[...])
    for z4 in range(4):
        rows = [flat[z4 * 32 + (n % 2) * 16 + (n // 2) * 8 :][0:8] for n in range(4)]
        for zq in range(4):
            out = rows[zq]
            for n in range(4):
                if n != zq:
                    out = jnp.where(quarter == n, pltpu.roll(rows[n], ((n - zq) * 32) % 128, axis=1), out)
            send2[zq * 4 + z4] = out[0:5]

    for at, dev in depth_peers:
        send(send2, at, recv2, z, 2, dev)
    recv2[z] = send2[z]

    for f in range(9):
        shrink = one_hot(row16 == (lane16 // 16) * 16 + SEAT[f])
        for n in range(2):
            fold[:, (f * 2 + n) * 128 : (f * 2 + n + 1) * 128] = shrink
    lower = one_hot(lane16 < row16)
    upper = one_hot(lane16 > row16)
    lower = jnp.concatenate([lower, lower], axis=1)
    upper = jnp.concatenate([upper, upper], axis=1)
    across = jnp.zeros((128, 128), F32)
    down_rows = iota((32, 48), 1) - iota((32, 48), 0) - 3
    down_band = jnp.zeros((32, 48), F32)
    back_rows = iota((16, 32), 0) + 13 - iota((16, 32), 1)
    back_band = jnp.zeros((16, 32), F32)
    for n in range(11):
        across = jnp.where(row16 - lane16 + 5 == n, WINDOW_TAPS[n], across)
        down_band = jnp.where(down_rows == n, WINDOW_TAPS[n], down_band)
        back_band = jnp.where(back_rows == n, WINDOW_TAPS[n], back_band)

    def blur(images):
        tall = dot_exact(down_band, jnp.concatenate(images, axis=1))
        n = len(images)
        flat = jnp.concatenate([tall[:, i * 128 : (i + 1) * 128] for i in range(n)], axis=0)
        flat = dot_exact(flat, across)
        return [flat[i * 32 : (i + 1) * 32] for i in range(n)]

    def with_halo(halo, n, own):
        above = jnp.where(s > 0, halo[n], 0.0)
        below = jnp.where(s < 127, halo[3 + n], 0.0)
        return jnp.concatenate([above, own, below], axis=0)

    wait_bytes(halo_y, 6, rsem.at[1])
    ys = [with_halo(halo_y, n, target_ref[n]) for n in range(3)]
    y_stats = blur(ys + [v * v for v in ys])
    live = jnp.broadcast_to(cnt_ref[:, 7:8], (128, 128))
    for t in range(7):
        live = jnp.where(lane16 // 16 == t, cnt_ref[:, t : t + 1], live)
    live = row16 < live

    wait_bytes(recv2, 15, rsem.at[2])

    got_z = [jnp.concatenate([recv2[n], jnp.zeros((3, 128), F32)], axis=0) for n in range(16)]
    tiles = []
    for t in range(8):
        block = jnp.broadcast_to(block_of[t : t + 1], (8, 128))
        lanes = jnp.broadcast_to(lane_in[t : t + 1], (8, 128))
        for half in range(2):
            got = take_lanes(got_z[0], lanes + half * 64)
            for n in range(1, 16):
                got = jnp.where(block == n, take_lanes(got_z[n], lanes + half * 64), got)
            tiles.append(got)
    listed = jnp.transpose(jnp.concatenate(tiles, axis=0))
    wide = [take_lanes(listed, (lane16 // 16) * 16 + SEAT[f]) for f in range(10)]
    dx = wide[0] - (lane16.astype(F32) + 0.5)
    ca, cb, cc, op = wide[2:6]
    fsc[0] = wide[1]
    fsc[1] = jnp.where(live, -0.5 * ca * dx * dx, -1e30)
    fsc[2] = cb * dx
    fsc[3] = 0.5 * cc
    fsc[4] = op
    for f in range(4):
        fsc[5 + f] = wide[6 + f]
    fsc[9] = ca * dx
    fsc[10] = cb
    fsc[11] = dx
    first_row = (s * TILE).astype(F32) + 0.5

    for i in range(4):
        keeps = []
        for row in range(i * 4, i * 4 + 4):
            dy = fsc[0] - (first_row + float(row))
            raw = fsc[4] * jnp.exp(fsc[1] - dy * (fsc[2] + fsc[3] * dy))
            raws[row] = raw
            keeps.append(jnp.concatenate(split(jnp.log(1.0 - jnp.minimum(raw, ALPHA_MAX)), 2), axis=0))
        t4 = jnp.exp(dot(lower, jnp.concatenate(keeps, axis=1)))
        for n in range(4):
            row = i * 4 + n
            t = t4[:, n * 128 : (n + 1) * 128]
            w = jnp.minimum(raws[row], ALPHA_MAX) * t
            trans[row] = t
            weights[row] = w
            for f in range(4):
                image[f, row : row + 1, :] = jnp.sum(w * fsc[5 + f], axis=0, keepdims=True)

    send(image, pl.ds(0, 3), halo_x, pl.ds(0, 3), 3, (down, y))
    send(image, pl.ds(0, 3), halo_x, pl.ds(3, 3), 3, (up, y))
    stores[1].start()
    stores[2].start()

    def factor_rows(row, carry):
        raw = raws[row]
        moved = jnp.where(raw < ALPHA_MAX, raw, jnp.where(raw == ALPHA_MAX, 0.5 * raw, 0.0))
        raws[row] = moved / (1.0 - jnp.minimum(raw, ALPHA_MAX))
        trans[row] = trans[row] * moved
        return carry

    lax.fori_loop(0, 16, factor_rows, 0)
    wait_bytes(halo_x, 6, rsem.at[3])
    xs = [with_halo(halo_x, n, image[n]) for n in range(3)]
    x_stats = blur(xs + [v * v for v in xs] + [xs[n] * ys[n] for n in range(3)])
    grow = s * TILE - 8 + iota((32, 128), 0)
    share = jnp.where((grow >= 0) & (grow < height), -STRUCTURE_WEIGHT / (TILE * TILE), 0.0)
    pulls = []
    for n in range(3):
        mx, exx, exy = x_stats[n], x_stats[3 + n], x_stats[6 + n]
        my, eyy = y_stats[n], y_stats[3 + n]
        a1 = 2.0 * mx * my + STABLE_MEAN
        a2 = 2.0 * (exy - mx * my) + STABLE_SPREAD
        b1 = mx * mx + my * my + STABLE_MEAN
        b2 = (exx - mx * mx) + (eyy - my * my) + STABLE_SPREAD
        inv = share / (b1 * b2)
        ssim = a1 * a2 / (b1 * b2)
        d_exy = 2.0 * a1 * inv
        d_exx = -ssim * b1 * inv
        d_mx = 2.0 * (my * (a2 - a1) * inv - ssim * mx * (b2 - b1) * inv)
        pulls.append((d_mx, d_exx, d_exy))
    nine = [pulls[n][i] for i in range(3) for n in range(3)]
    tall = dot_exact(back_band, jnp.concatenate(nine, axis=1))
    flat = dot_exact(jnp.concatenate([tall[:, i * 128 : (i + 1) * 128] for i in range(9)], axis=0), across)
    for n in range(3):
        vx, vy = image[n], target_ref[n]
        diff = vx - vy
        smooth = (1.0 - STRUCTURE_WEIGHT) / (TILE * TILE) * diff / jnp.sqrt(diff * diff + SMOOTHING**2)
        b_mx, b_xx, b_xy = (flat[(i * 3 + n) * 16 : (i * 3 + n + 1) * 16] for i in range(3))
        gimage[n] = b_mx + 2.0 * vx * b_xx + vy * b_xy + smooth

    sums = [0.0] * 6
    for i in range(4):
        dws, products = [], []
        for row in range(i * 4, i * 4 + 4):
            dw = sum(gimage[f, row : row + 1, :] * fsc[5 + f] for f in range(3))
            dws.append(dw)
            products.append(jnp.concatenate(split(dw * weights[row], 2), axis=0))
        later = dot(upper, jnp.concatenate(products, axis=1))
        for n in range(4):
            row = i * 4 + n
            d_power = dws[n] * trans[row] - later[:, n * 128 : (n + 1) * 128] * raws[row]
            moved = d_power * (fsc[0] - (first_row + float(row)))
            dy = fsc[0] - (first_row + float(row))
            terms = [d_power, moved, moved * dy]
            terms += [weights[row] * gimage[f, row : row + 1, :] for f in range(3)]
            sums = [a + b for a, b in zip(sums, terms)]
    s0, s1, s2 = sums[0:3]
    adx, cb, dx = fsc[9], fsc[10], fsc[11]
    grads = [
        -(adx * s0 + cb * s1),
        -(2.0 * fsc[3] * s1 + fsc[2] * s0),
        -0.5 * dx * dx * s0,
        -dx * s1,
        -0.5 * s2,
        s0 / fsc[4],
        sums[3],
        sums[4],
        sums[5],
    ]
    parts = [part for f in range(9) for part in split(grads[f], 2)]
    turned = lax.dot_general(
        fold[...], jnp.concatenate(parts, axis=1), (((1,), (1,)), ((), ())), preferred_element_type=F32
    )
    for n in range(16):
        tile = jnp.broadcast_to(tile_from[n : n + 1], (8, 128))
        lanes = jnp.broadcast_to(entry_from[n : n + 1], (8, 128))
        halves = []
        for half in range(2):
            put = take_lanes(turned[half * 8 : half * 8 + 8], lanes)
            for t in range(1, 8):
                at = t * 16 + half * 8
                put = jnp.where(tile == t, take_lanes(turned[at : at + 8], lanes), put)
            halves.append(put)
        back2s[n] = jnp.where(quarter < 2, halves[0], halves[1])[0:5]

    for at, dev in depth_peers:
        send(back2s, at, back2r, z, 4, dev)
    back2r[z] = back2s[z]
    _, pull = jax.vjp(
        lambda *a: geometry(*a, camera, height, columns)[2:5], center, log_scale, quaternion
    )
    one, none = jnp.ones((8, 128), F32), jnp.zeros((8, 128), F32)
    jac = []
    for i in range(3):
        d_center, d_scale, d_turn = pull(tuple(one if i == n else none for n in range(3)))
        jac += list(d_center) + list(d_scale) + list(d_turn)
    passed = [jnp.where(v > 0.0, 1.0, jnp.where(v == 0.0, 0.5, 0.0)) for v in raw_colors]
    for ch in range(3):
        _, pull = jax.vjp(lambda a: raw_color(har, directions(a, camera), ch), center)
        jac += [passed[ch] * v for v in pull(one)[0]]
    shift = [center[i] - camera[i] for i in range(2)]
    jac += [FOCAL_LENGTH * iz] + [-FOCAL_LENGTH * v * iz * iz for v in shift]
    jac += [opaque * (1.0 - opaque)]

    columns_of = jnp.transpose(jnp.concatenate([number.astype(F32)] * 64, axis=0)).astype(jnp.int32)
    total = jnp.zeros((32, 128), F32)
    for j in range(2):
        hit = chunk_of[j][0:32] == iota((32, 128), 0)
        value = jnp.where(hit, (iota((32, 128), 1) + (1 + j * 128)).astype(F32), 0.0).astype(BF16)
        total = total + dot(value, one_hot(columns_of[:, j : j + 1] % 128 == lane128))
    inv_ref[...] = total.astype(jnp.int32)
    stores[0].start()
    wait_bytes(back2r, 15, rsem.at[4])
    back_z = [jnp.concatenate([back2r[n], jnp.zeros((3, 128), F32)], axis=0) for n in range(16)]
    for z4 in range(4):
        for n in range(4):
            out = back_z[n * 4 + z4]
            for zq in range(4):
                if zq != n:
                    moved = pltpu.roll(back_z[zq * 4 + z4], ((zq - n) * 32) % 128, axis=1)
                    out = jnp.where(quarter == zq, moved, out)
            at = z4 * 32 + (n % 2) * 16 + (n // 2) * 8
            turn[at : at + 8, :] = out
    turn[...] = jnp.transpose(turn[...])
    for zq in range(4):
        for w in range(4):
            back1s[w * 8 : (w + 1) * 8, zq, :] = turn[zq * 32 + w * 8 : zq * 32 + w * 8 + 8, :]
    for at, dev in ring_peers:
        send(back1s, at, back1r, me, 5, dev)
    back1r[me] = back1s[me]
    wait_bytes(back1r, 31, rsem.at[5])
    for a in range(4):
        rows = [
            jnp.concatenate([back1r[v * 8 + 2 * a], back1r[v * 8 + 2 * a + 1]], axis=0) for v in range(4)
        ]
        for z4 in range(4):
            out = rows[z4]
            for v in range(4):
                if v != z4:
                    moved = pltpu.roll(rows[v], ((v - z4) * 32) % 128, axis=1)
                    out = jnp.where(quarter == v, moved, out)
            for n in range(2):
                sq[pl.ds(a * 32 + n + z4 * 2, 4, stride=8), :] = out[n * 4 : n * 4 + 4]
    turn[...] = jnp.transpose(sq[...])
    du, dr, da, db, dc, do, *dcol = [turn[pl.ds(SEAT[f], 8, stride=16), :] for f in range(9)]
    conic = (da, db, dc)
    geo = [sum(conic[i] * jac[i * 10 + n] for i in range(3)) for n in range(10)]
    for n in range(3):
        geo[n] = geo[n] + sum(dcol[ch] * jac[30 + ch * 3 + n] for ch in range(3))
    ja, jx, jy, d_opaque = jac[39:43]
    geo[0] = geo[0] + du * ja
    geo[1] = geo[1] + dr * ja
    geo[2] = geo[2] + du * jx + dr * jy
    shown = [dcol[ch] * passed[ch] for ch in range(3)]
    rows = [shown[ch] * basis[i] for ch in range(3) for i in range(16)] + geo + [do * d_opaque]
    for i in range(59):
        rows_ref[i * 8 : (i + 1) * 8, :] = rows[i]
    for i in range(59, 64):
        rows_ref[i * 8 : (i + 1) * 8, :] = none
    for j in range(2):
        grad_ref[j] = sum(rows_ref[pl.ds(v * 2 + j, 64, stride=8), :] for v in range(4))
    stores[3].start()

    wait_bytes(send1, 31, ssem.at[0])
    wait_bytes(halo_y, 6, ssem.at[1])
    wait_bytes(send2, 15, ssem.at[2])
    wait_bytes(halo_x, 6, ssem.at[3])
    wait_bytes(back2s, 15, ssem.at[4])
    wait_bytes(back1s, 31, ssem.at[5])
    for store in stores:
        store.wait()


def owner_kernel(
    grad_in, inv_in, rend_in, depth_in,
    har_hbm, cen_hbm, lsc_hbm, rot_hbm, opa_hbm, rend_hbm, depth_hbm,
    grad_ref, inv_ref, har_ref, cen_ref, lsc_ref, rot_ref, opa_ref, sem,
):
    loads = [
        pltpu.make_async_copy(grad_in, grad_ref, sem.at[22]),
        pltpu.make_async_copy(inv_in, inv_ref, sem.at[43]),
    ]
    copies = [
        pltpu.make_async_copy(rend_in, rend_hbm, sem.at[0]),
        pltpu.make_async_copy(depth_in, depth_hbm, sem.at[1]),
    ]
    for copy in loads + copies:
        copy.start()
    for load in loads:
        load.wait()
    halves = [grad_ref[j] for j in range(2)]
    count = har_hbm.shape[1]
    pieces = 8
    wide = count // pieces
    for piece in range(pieces):
        for h in range(piece * wide // 128, (piece + 1) * wide // 128):
            at = slice(h * 128, (h + 1) * 128)
            number = jnp.broadcast_to(inv_ref[h : h + 1, :], (64, 128))
            lanes = (number + 127) % 128
            out = jnp.where(number > 128, take_lanes(halves[1], lanes), take_lanes(halves[0], lanes))
            out = jnp.where(number > 0, out, 0.0)
            har_ref[:, at] = out[0:48]
            cen_ref[:, at] = out[48:51]
            lsc_ref[:, at] = out[51:54]
            rot_ref[:, at] = out[54:58]
            opa_ref[:, at] = out[58:59]
        part = pl.ds(piece * wide, wide)
        for n, (source, target) in enumerate((
            (har_ref, har_hbm), (cen_ref, cen_hbm), (lsc_ref, lsc_hbm), (rot_ref, rot_hbm), (opa_ref, opa_hbm)
        )):
            copy = pltpu.make_async_copy(source.at[:, part], target.at[:, part], sem.at[2 + piece * 5 + n])
            copy.start()
            copies.append(copy)
    for copy in copies:
        copy.wait()


def on_device(
    centers, log_scales, rotations, opacity, harmonics, cameras, send_index, tile_lists, counts, target
):
    strips = lax.axis_size("space")
    height = TILE * strips
    columns = target.shape[-1]
    count = centers.shape[1]
    hbm = pl.BlockSpec(memory_space=pltpu.HBM)
    index = jnp.swapaxes(send_index, 2, 3).reshape(2, strips)
    dma = pltpu.SemaphoreType.DMA

    def shape(*dims):
        return jax.ShapeDtypeStruct(dims, F32)

    params = [VMEM((48, count), F32), VMEM((3, count), F32), VMEM((3, count), F32), VMEM((4, count), F32), VMEM((1, count), F32)]
    rendered, inverse_depth, inverse, grads = pl.pallas_call(
        functools.partial(step_kernel, height, columns),
        out_shape=[
            shape(3, 16, 128),
            shape(16, 128),
            jax.ShapeDtypeStruct((32, 128), jnp.int32),
            shape(2, 64, 128),
        ],
        in_specs=[hbm] * 10,
        out_specs=[hbm] * 4,
        scratch_shapes=params + [
            VMEM((4, 3), F32),
            VMEM((2, 128), jnp.int32),
            VMEM((8, 128), jnp.int32),
            VMEM((1, 8), jnp.int32),
            VMEM((3, 16, 128), F32),
            VMEM((16, count), F32),
            VMEM((128, 128), F32),
            VMEM((128, 128), F32),
            VMEM((32, 4, 128), F32),
            VMEM((32, 4, 128), F32),
            VMEM((16, 5, 128), F32),
            VMEM((16, 5, 128), F32),
            VMEM((128, 2304), BF16),
            VMEM((6, 16, 128), F32),
            VMEM((6, 16, 128), F32),
            VMEM((16, 128, 128), F32),
            VMEM((16, 128, 128), F32),
            VMEM((16, 128, 128), F32),
            VMEM((16, 128, 128), F32),
            VMEM((256, 2048), BF16),
            VMEM((4, 16, 128), F32),
            VMEM((3, 16, 128), F32),
            VMEM((12, 128, 128), F32),
            VMEM((16, 5, 128), F32),
            VMEM((16, 5, 128), F32),
            VMEM((32, 4, 128), F32),
            VMEM((32, 4, 128), F32),
            VMEM((32, 128), jnp.int32),
            VMEM((512, 128), F32),
            VMEM((2, 64, 128), F32),
            VMEM((128, 128), F32),
            dma((14,)),
            dma((6,)),
            dma((6,)),
        ],
        compiler_params=pltpu.CompilerParams(
            collective_id=0, has_side_effects=True, vmem_limit_bytes=60 * 2**20
        ),
        name="render_step",
    )(
        harmonics.reshape(48, count),
        centers,
        log_scales,
        rotations,
        opacity.reshape(1, count),
        cameras,
        index,
        tile_lists[0],
        counts,
        target[0],
    )
    d_har, d_cen, d_lsc, d_rot, d_opa, rendered, inverse_depth = pl.pallas_call(
        owner_kernel,
        out_shape=[
            shape(48, count), shape(3, count), shape(3, count), shape(4, count), shape(1, count),
            shape(3, 16, 128), shape(16, 128),
        ],
        in_specs=[hbm] * 4,
        out_specs=[hbm] * 7,
        scratch_shapes=[
            VMEM((2, 64, 128), F32),
            VMEM((32, 128), jnp.int32),
        ]
        + params
        + [dma((44,))],
        compiler_params=pltpu.CompilerParams(vmem_limit_bytes=60 * 2**20),
        name="owner_pull",
    )(grads, inverse, rendered, inverse_depth)
    return (
        rendered[None],
        inverse_depth[None],
        d_cen,
        d_lsc,
        d_rot,
        d_opa.reshape(count),
        d_har.reshape(3, 16, count),
    )


def solution(mesh):
    return jax.shard_map(
        on_device,
        mesh=mesh,
        in_specs=(
            P(None, ("space", "view")),
            P(None, ("space", "view")),
            P(None, ("space", "view")),
            P(("space", "view")),
            P(None, None, ("space", "view")),
            P(),
            P("space", "view", None, None),
            P("space", None, None),
            P("space", None),
            P("view", None, "space", None),
        ),
        out_specs=(
            P("view", None, "space", None),
            P("view", "space", None),
            P(None, ("space", "view")),
            P(None, ("space", "view")),
            P(None, ("space", "view")),
            P(("space", "view")),
            P(None, None, ("space", "view")),
        ),
        check_vma=False,
    )
```
